32 devices in a mesh: seq: 4 (over y, x), mem: 8 (over z, core).
Axes of the slice: x: 2, y: 2, z: 4, core: 2. Of those that a mesh axis runs over, the one named last changes fastest.
Arguments:
- query: bfloat16 [4096, 2048], P(('seq', 'mem')), may hold values from -64 to 64
- key: bfloat16 [4096, 2048], P(('seq', 'mem')), may hold values from -64 to 64
- value: bfloat16 [4096, 2048], P(('seq', 'mem')), may hold values from -6 to 6
- mem_key: bfloat16 [1024, 2048], P('mem'), may hold values from -6 to 6
- mem_value: bfloat16 [1024, 2048], P('mem'), may hold values from -6 to 6
- block_ids: int32 [512, 2], P(('seq', 'mem')), may hold values from 0 to 7, all different within a row; in each aligned block of 16 rows (0 to 15, 16 to 31, ...) at most 8 rows name the same one
- gate_logit: float32 [16], replicated, may hold values from -2 to 2
- d_out: bfloat16 [4096, 2048], P(('seq', 'mem')), may hold values from -16 to 16
Outputs:
- out: bfloat16 [4096, 2048], P(('seq', 'mem'))
- d_query: bfloat16 [4096, 2048], P(('seq', 'mem'))
- gate_grad: float32 [16], replicated
The draws below stay inside these ranges and needn't reach their ends.
Inputs may be any that keep to these rules, and one draw needn't show every extreme that they name: `block_ids`: each row names 2 different memory blocks. Among the query groups of one device no block is named by more than 8 rows, and some device names some block exactly 8 times.
All inputs are finite; a program needn't handle non-finite values.
Results may differ from the reference program's by a relative error of at most 0.015.
Values may be sent and summed in bfloat16 or wider, within the bound.
No kernel may reach another device: no remote copies, remote signals or barrier semaphores. Data moves between devices by JAX's collectives and lax.ppermute only.
A program may use at most 64 MiB of HBM per device.

```python
import math
import jax
import jax.numpy as jnp
import numpy as np
from jax import lax

HEADS = 16
HEAD_DIM = 128
QBLK = 8
TOPB = 2
MROWS = 128
T_DEV = 128
WIDTH = 2048
TOKENS = 4096
NQG = 512
MEM_ROWS = 1024
CAP = 8
N_MEM = 8


def draw_query(key, part):
    key = jax.random.fold_in(key, 7)
    drawn = jax.random.normal(key, (TOKENS, HEADS * HEAD_DIM), jnp.float32)
    return jnp.clip(drawn, -64.0, 64.0).astype(jnp.bfloat16)


def draw_key(key, part):
    key = jax.random.fold_in(key, 8)
    drawn = jax.random.normal(key, (TOKENS, HEADS * HEAD_DIM), jnp.float32)
    return jnp.clip(drawn, -64.0, 64.0).astype(jnp.bfloat16)


def draw_d_out(key, part):
    key = jax.random.fold_in(key, 9)
    rows_all = jnp.arange(TOKENS).astype(jnp.float32) / TOKENS
    drawn = jnp.clip(jax.random.normal(key, (TOKENS, HEADS * HEAD_DIM), jnp.float32), -5.0, 5.0)
    drawn = drawn * (3.0 ** rows_all)[:, None]
    return drawn.astype(jnp.bfloat16)


def levels(rng, dims, pieces, smallest, top_value):
    level = 1.0
    for position, parts in pieces:
        heights = jax.random.uniform(jax.random.fold_in(jax.random.fold_in(rng, 6), position), (parts,), jnp.float32, smallest / len(pieces), top_value / len(pieces))
        level = level * jnp.repeat(jnp.exp(heights), dims[position] // parts).reshape((-1,) + (1,) * (len(dims) - 1 - position))
    return level


def shared_out(rng, own, number, rows, amount, top, reach, lean):
    sequence = jax.random.permutation(rng, amount)
    heavy_load, common = shares(amount, rows * top, reach, lean, True), shares(amount, rows * top, reach, lean, False)
    places = jnp.arange(amount)

    def named(tallies, turn):
        used = int((tallies > 0).sum())
        fixed = max(1, used // 4)
        shifted = fixed + (places - fixed + turn * (used - fixed)) % max(1, amount - fixed)
        return jnp.zeros((amount,), jnp.int32).at[sequence[jnp.where(places < fixed, places, shifted)]].set(jnp.asarray(tallies, jnp.int32))

    tallies = jnp.where(number % 4 == 0, named(heavy_load, number // 4), named(common, number - number // 4 - 1))
    mixed = jax.random.permutation(jax.random.fold_in(own, 3), amount)
    giver, sink = mixed[0:amount // 2 * 2:2], mixed[1:amount // 2 * 2:2]
    room = jnp.minimum(tallies[giver] - 1, reach - tallies[sink]) // 2
    room = jnp.where((giver == sequence[0]) | (sink == sequence[0]) | (tallies[sink] == 0), 0, jnp.maximum(room, 0))
    shifted = jax.random.randint(jax.random.fold_in(own, 4), (amount // 2,), 0, 1 << 20) % (room + 1)
    tallies = tallies.at[giver].add(-shifted).at[sink].add(shifted)
    items = jnp.searchsorted(jnp.cumsum(tallies), jnp.arange(rows * top), side="right").astype(jnp.int32)
    table = items.reshape(top, rows).T
    table = table[jax.random.permutation(jax.random.fold_in(own, 1), rows)]
    turn = jax.random.randint(jax.random.fold_in(own, 2), (rows, 1), 0, top)
    return jnp.take_along_axis(table, (jnp.arange(top)[None, :] + turn) % top, axis=1)


def shares(amount, total, bound, lean, full):
    loads = [(1 << 20) // math.isqrt(grade ** lean) + 1 for grade in range(1, amount + 1)]
    largest = bound if full else min(bound, max(-(-total // amount), total * loads[0] // sum(loads)))
    least = 1 if total - largest >= amount - 1 else 0
    counts, surplus = [largest] + [least] * (amount - 1), total - largest - least * (amount - 1)
    while surplus > 0:
        free = [i for i in range(1, amount) if counts[i] < largest] or [i for i in range(1, amount) if counts[i] < bound]
        mass, budget = sum([loads[i] for i in free]), surplus
        for i in free:
            extra = min(bound - counts[i], max(1, budget * loads[i] // mass), surplus)
            counts[i] = counts[i] + extra
            surplus = surplus - extra
    return np.array(counts)


def scatter_about(key, extent, deviation, bound, shards=(), kind=jnp.bfloat16):
    entries = jax.random.normal(key, extent, jnp.float32) * deviation
    if len(shards) > 0:
        entries = levels(key, extent, shards, -0.22, 0.18) * entries
    return jnp.clip(entries, min=-bound, max=bound).astype(kind)


def setup_inputs(seed: int = 0) -> dict:
    key_of = jax.random.split(jax.random.key(seed), 9)
    query = draw_query(jax.random.fold_in(key_of[8], 71), 0)
    key = draw_key(jax.random.fold_in(key_of[8], 71), 0)
    value = scatter_about(key_of[2], (TOKENS, WIDTH), 1.0, 6.0, ((0, 32),))
    mem_key = scatter_about(key_of[3], (MEM_ROWS, WIDTH), 1.0, 6.0, ((0, 8),))
    mem_value = scatter_about(key_of[4], (MEM_ROWS, WIDTH), 1.0, 6.0, ((0, 8),))
    block_ids_keys = jax.random.split(jax.random.fold_in(key_of[5], 1), NQG // (T_DEV // QBLK))
    block_ids_turns = jax.random.permutation(jax.random.fold_in(key_of[5], 3), NQG // (T_DEV // QBLK))
    block_ids = jax.vmap(lambda own, number: shared_out(jax.random.fold_in(key_of[5], 2), own, number, T_DEV // QBLK, N_MEM, TOPB, CAP, 2))(block_ids_keys, block_ids_turns).reshape((NQG, TOPB))
    gate_logit = jnp.clip(jax.random.uniform(key_of[6], (HEADS,), jnp.float32, -2.0, 2.0), -2.0, 2.0)
    d_out = draw_d_out(jax.random.fold_in(key_of[8], 71), 0)
    return dict(query=query, key=key, value=value, mem_key=mem_key, mem_value=mem_value, block_ids=block_ids, gate_logit=gate_logit, d_out=d_out)


def reference(query, key, value, mem_key, mem_value, block_ids, gate_logit, d_out):
    softmax_scale = HEAD_DIM ** (-0.5)
    groups = T_DEV // QBLK
    block_count = TOKENS // T_DEV
    gate_open = jax.nn.sigmoid(gate_logit.astype(jnp.float32))
    gate_col = gate_open[None, :, None]
    mem_k_blocks = mem_key.reshape(N_MEM, MROWS, HEADS, HEAD_DIM)
    mem_v_blocks = mem_value.reshape(N_MEM, MROWS, HEADS, HEAD_DIM)
    rows_idx = lax.broadcasted_iota(jnp.int32, (T_DEV, T_DEV), 0)
    cols_idx = lax.broadcasted_iota(jnp.int32, (T_DEV, T_DEV), 1)
    causal_mask = rows_idx >= cols_idx

    def one_block(inputs):
        q_block, k_block, v_block, g_block, id_block = inputs
        q_heads = q_block.reshape(T_DEV, HEADS, HEAD_DIM).astype(jnp.float32)
        k_heads = k_block.reshape(T_DEV, HEADS, HEAD_DIM).astype(jnp.float32)
        v_heads = v_block.reshape(T_DEV, HEADS, HEAD_DIM).astype(jnp.float32)
        grad_f = g_block.reshape(T_DEV, HEADS, HEAD_DIM).astype(jnp.float32)
        local_scores = jnp.einsum('qhd,khd->hqk', q_heads, k_heads) * softmax_scale
        local_scores = jnp.where(causal_mask[None], local_scores, -1e+30)
        local_peak = lax.optimization_barrier(jnp.max(local_scores, axis=-1, keepdims=True))
        local_exp = jnp.exp(local_scores - local_peak)
        local_prob = local_exp / lax.optimization_barrier(jnp.sum(local_exp, axis=-1, keepdims=True))
        local_weight = lax.optimization_barrier(local_prob.astype(jnp.bfloat16)).astype(jnp.float32)
        local_out = jnp.einsum('hqk,khd->qhd', local_weight, v_heads)
        picked_k = mem_k_blocks[id_block].astype(jnp.float32)
        picked_v = mem_v_blocks[id_block].astype(jnp.float32)
        q_groups = q_heads.reshape(groups, QBLK, HEADS, HEAD_DIM)
        pair_scores = jnp.einsum('gqhd,gtkhd->gthqk', q_groups, picked_k) * softmax_scale
        pair_peak = lax.optimization_barrier(jnp.max(pair_scores, axis=-1, keepdims=True))
        pair_lse = pair_peak + jnp.log(lax.optimization_barrier(jnp.sum(jnp.exp(pair_scores - pair_peak), axis=-1, keepdims=True)))
        pair_weight = lax.optimization_barrier(jnp.exp(pair_scores - pair_lse).astype(jnp.bfloat16)).astype(jnp.float32)
        pair_out = jnp.einsum('gthqk,gtkhd->gtqhd', pair_weight, picked_v)
        pair_out = lax.optimization_barrier(pair_out.astype(jnp.bfloat16)).astype(jnp.float32)
        lse_peak = lax.optimization_barrier(jnp.max(pair_lse, axis=1, keepdims=True))
        total_lse = lse_peak + jnp.log(lax.optimization_barrier(jnp.sum(jnp.exp(pair_lse - lse_peak), axis=1, keepdims=True)))
        pair_share = jnp.exp(pair_lse - total_lse)
        share_view = jnp.transpose(pair_share[..., 0], (0, 1, 3, 2))[..., None]
        mem_out = lax.optimization_barrier(jnp.sum(share_view * pair_out, axis=1)).reshape(T_DEV, HEADS, HEAD_DIM)
        mixed = gate_col * mem_out + (1.0 - gate_col) * local_out
        out_block = mixed.astype(jnp.bfloat16).reshape(T_DEV, HEADS * HEAD_DIM)
        gate_term = lax.optimization_barrier(jnp.sum(grad_f * (mem_out - local_out), axis=(0, 2)))
        local_dout = lax.optimization_barrier(((1.0 - gate_col) * grad_f).astype(jnp.bfloat16)).astype(jnp.float32)
        local_delta = lax.optimization_barrier(jnp.sum(local_dout * local_out, axis=-1))
        local_dp = jnp.einsum('qhd,khd->hqk', local_dout, v_heads)
        local_ds = local_prob * (local_dp - jnp.transpose(local_delta)[:, :, None])
        local_ds = lax.optimization_barrier(local_ds.astype(jnp.bfloat16)).astype(jnp.float32)
        local_dq = jnp.einsum('hqk,khd->qhd', local_ds, k_heads) * softmax_scale
        mem_dout = lax.optimization_barrier((gate_col * grad_f).astype(jnp.bfloat16)).astype(jnp.float32)
        mem_delta = lax.optimization_barrier(jnp.sum(mem_dout * mem_out, axis=-1))
        dout_groups = mem_dout.reshape(groups, QBLK, HEADS, HEAD_DIM)
        delta_view = jnp.transpose(mem_delta.reshape(groups, QBLK, HEADS), (0, 2, 1))[:, None, :, :, None]
        pair_prob = jnp.exp(pair_scores - total_lse)
        pair_dp = jnp.einsum('gqhd,gtkhd->gthqk', dout_groups, picked_v)
        mem_ds = lax.optimization_barrier((pair_prob * (pair_dp - delta_view)).astype(jnp.bfloat16)).astype(jnp.float32)
        pair_dq = jnp.einsum('gthqk,gtkhd->gtqhd', mem_ds, picked_k) * softmax_scale
        pair_dq = lax.optimization_barrier(pair_dq.astype(jnp.bfloat16)).astype(jnp.float32)
        mem_dq = lax.optimization_barrier(jnp.sum(pair_dq, axis=1)).reshape(T_DEV, HEADS, HEAD_DIM)
        dq_block = (local_dq + mem_dq).astype(jnp.bfloat16).reshape(T_DEV, HEADS * HEAD_DIM)
        return (out_block, dq_block, gate_term)
    stacked = (query.reshape(block_count, T_DEV, HEADS * HEAD_DIM), key.reshape(block_count, T_DEV, HEADS * HEAD_DIM), value.reshape(block_count, T_DEV, HEADS * HEAD_DIM), d_out.reshape(block_count, T_DEV, HEADS * HEAD_DIM), block_ids.reshape(block_count, groups, TOPB).astype(jnp.int32))
    out_blocks, dq_blocks, gate_terms = lax.map(one_block, stacked)
    gate_grad = lax.optimization_barrier(jnp.sum(gate_terms, axis=0)) * gate_open * (1.0 - gate_open) / math.sqrt(TOKENS)
    out = out_blocks.reshape(TOKENS, HEADS * HEAD_DIM)
    d_query = dq_blocks.reshape(TOKENS, HEADS * HEAD_DIM)
    return (out, d_query, gate_grad)
```

```python
import functools
import math

import jax
import jax.numpy as jnp
from jax import lax
from jax.experimental import pallas as pl
from jax.experimental.pallas import tpu as pltpu
from jax.sharding import Mesh, PartitionSpec as P

HEAD_DIM = 128
PAIR = 2
CHUNK = PAIR * HEAD_DIM
TILE = 2
NEG = -1e30
LOG2E = math.log2(math.e)
MIB = 1024 * 1024
F32 = jnp.float32
BF16 = jnp.bfloat16
NT = (((1,), (1,)), ((), ()))
NN = (((1,), (0,)), ((), ()))
PLANE = ("sb", "core")
MEM = ("z", "core")
ALL = ("sa", "sb", "z", "core")


def dot(a, b, dims=NN):
    return lax.dot_general(a, b, dims, preferred_element_type=F32)


def head_cols(h):
    return slice(h * HEAD_DIM, (h + 1) * HEAD_DIM)


def chunk_columns(chunk):
    return pl.ds(pl.multiple_of(chunk * CHUNK, CHUNK), CHUNK)


def plane_index():
    return lax.axis_index("sb") * 2 + lax.axis_index("core")


def row_sums(x):
    high = x.astype(BF16)
    low = (x - high.astype(F32)).astype(BF16)
    return dot(jnp.concatenate([high, low], axis=1), jnp.ones((2 * HEAD_DIM, HEAD_DIM), BF16))


def prologue_kernel(
    blocks, mk_hbm, mv_hbm, q_hbm, g_hbm, ids_ref, both_ref, *refs
):
    *out_refs, mem_sems, in_sems = refs
    tok = q_hbm.shape[0]
    fetched, groups = ids_ref.shape
    chunk = plane_index()
    copies = [
        pltpu.make_async_copy(
            ref.at[:, chunk_columns(chunk ^ i)], both_ref.at[i, t], mem_sems.at[i, t]
        )
        for i in range(2)
        for t, ref in enumerate((mk_hbm, mv_hbm))
    ]
    for k, out_ref in enumerate(out_refs):
        for t, ref in enumerate((q_hbm, g_hbm)):
            span = slice(t * tok, (t + 1) * tok)
            copies.append(
                pltpu.make_async_copy(
                    ref.at[:, chunk_columns(chunk ^ k)], out_ref.at[span], in_sems.at[k, t]
                )
            )
    for copy in copies:
        copy.start()
    row = lax.broadcasted_iota(jnp.int32, (out_refs[0].shape[0] - 2 * tok, groups), 0)
    owner = lax.axis_index("z") * 2 + lax.axis_index("core")
    for core in range(2):
        hot = row >= blocks
        for t in range(fetched):
            hot = hot | (row == (ids_ref[t : t + 1, :] ^ owner ^ core))
        shun = jnp.where(hot, 0.0, 1.0).astype(BF16)
        for out_ref in out_refs[core::2]:
            out_ref[2 * tok :, :groups] = shun
    for copy in copies:
        copy.wait()


def local_forward_kernel(scale, q_ref, k_ref, v_ref, g_ref, out_ref, prob_ref, part_ref):
    tok = q_ref.shape[0]
    heads = part_ref.shape[1]
    row = lax.broadcasted_iota(jnp.int32, (tok, tok), 0)
    col = lax.broadcasted_iota(jnp.int32, (tok, tok), 1)
    causal = row >= col
    s = [dot(q_ref[:, head_cols(h)], k_ref[:, head_cols(h)], NT) for h in range(heads)]
    s = [jnp.where(causal, x, NEG) for x in s]
    e = [jnp.exp2((x - jnp.max(x, axis=1, keepdims=True)) * (scale * LOG2E)) for x in s]
    p = [x * (1.0 / row_sums(x)) for x in e]
    p = [x.astype(BF16) for x in p]
    for h in range(heads):
        cols = head_cols(h)
        o = dot(p[h], v_ref[:, cols])
        prob_ref[h] = p[h]
        out_ref[:, cols] = o
        part_ref[0, h : h + 1, :] = jnp.sum(g_ref[:, cols].astype(F32) * o, axis=0, keepdims=True)


def local_backward_kernel(scale, k_ref, v_ref, g_ref, gate_ref, out_ref, prob_ref, lo_ref, dq_ref):
    heads = prob_ref.shape[0]
    for h in range(heads):
        shut = 1.0 - gate_ref[:, head_cols(h)]
        lo_ref[:, head_cols(h)] = (shut * out_ref[:, head_cols(h)]).astype(BF16)
    dout = [
        ((1.0 - gate_ref[:, head_cols(h)]) * g_ref[:, head_cols(h)].astype(F32)).astype(BF16)
        for h in range(heads)
    ]
    delta = [row_sums(dout[h].astype(F32) * out_ref[:, head_cols(h)]) for h in range(heads)]
    dp = [dot(dout[h], v_ref[:, head_cols(h)], NT) for h in range(heads)]
    for h in range(heads):
        ds = (prob_ref[h].astype(F32) * (dp[h] - delta[h])).astype(BF16)
        dq_ref[:, head_cols(h)] = (dot(ds, k_ref[:, head_cols(h)]) * scale).astype(BF16)


def attend_kernel(scale, groups, peers, gate_ref, local_ref, *refs):
    *refs, k_all, v_all = refs
    got, mem_refs, back = refs[:peers], refs[peers:-peers], refs[-peers:]
    packet_rows = got[0].shape[0]
    blocks = len(mem_refs)
    rows = mem_refs[0].shape[2]
    heads = local_ref.shape[0]
    tok = (back[0].shape[0] - heads) // 2
    extra = packet_rows - 2 * tok
    chunk = plane_index()
    lane = lax.broadcasted_iota(jnp.int32, (rows, HEAD_DIM), 1)
    for h in range(PAIR):
        for b, ref in enumerate(mem_refs):
            span = slice(b * rows, (b + 1) * rows)
            k_all[h, span, :HEAD_DIM] = ref[b % 2, 0, :, head_cols(h)]
            k_all[h, span, HEAD_DIM:] = jnp.where(lane == b, NEG, 0.0).astype(BF16)
            v_all[h, span, :HEAD_DIM] = ref[b % 2, 1, :, head_cols(h)]
            v_all[h, span, HEAD_DIM:] = jnp.ones((rows, HEAD_DIM), BF16)
    spread = (
        lax.broadcasted_iota(jnp.int32, (tok, groups), 0) // (tok // groups)
        == lax.broadcasted_iota(jnp.int32, (tok, groups), 1)
    )
    spread = jnp.where(spread, 1.0, 0.0).astype(BF16)
    gates = gate_ref[:, chunk_columns(chunk)]
    pad = jnp.zeros((HEAD_DIM - extra, groups), BF16)

    def rows_of(first, start, cols):
        return jnp.concatenate(
            [got[first + t][start : start + tok, cols] for t in range(TILE)], axis=0
        )

    units = [(first, h) for first in range(0, peers, TILE) for h in range(PAIR)]
    shunned, scores, weights, parts = {}, {}, {}, [0.0] * PAIR
    for step in range(len(units) + 2):
        if step < len(units):
            first, h = units[step]
            if first not in shunned:
                shun = [
                    jnp.concatenate([got[first + t][2 * tok :, :groups], pad], axis=0)
                    for t in range(TILE)
                ]
                shunned[first] = jnp.concatenate(
                    [dot(spread, x, NT).astype(BF16) for x in shun], axis=0
                )
            q = jnp.concatenate([rows_of(first, 0, head_cols(h)), shunned[first]], axis=1)
            scores[step] = dot(q, k_all[h], NT)
        if 1 <= step <= len(units):
            u = step - 1
            first, h = units[u]
            gate = gates[:, head_cols(h)]
            s = scores.pop(u)
            peak = jnp.max(s, axis=1, keepdims=True)
            e = jnp.exp2((s - peak) * (scale * LOG2E)).astype(BF16)
            o = dot(e, v_all[h])
            inv = 1.0 / o[:, HEAD_DIM:]
            o = o[:, :HEAD_DIM] * inv
            g32 = rows_of(first, tok, head_cols(h)).astype(F32)
            dout = (gate * g32).astype(BF16)
            delta = row_sums(dout.astype(F32) * o)
            mixed = (gate * o).astype(BF16)
            for t in range(TILE):
                back[first + t][:tok, head_cols(h)] = mixed[t * tok : (t + 1) * tok]
            parts[h] = parts[h] + jnp.sum(g32 * o, axis=0, keepdims=True)
            weights[u] = (e, dout, delta, inv)
        if 2 <= step:
            u = step - 2
            first, h = units[u]
            e, dout, delta, inv = weights.pop(u)
            dp = dot(dout, v_all[h, :, :HEAD_DIM], NT)
            ds = (e.astype(F32) * (dp - jnp.concatenate([delta] * blocks, axis=1))).astype(BF16)
            dq = (dot(ds, k_all[h, :, :HEAD_DIM]) * (inv * scale)).astype(BF16)
            for t in range(TILE):
                back[first + t][tok : 2 * tok, head_cols(h)] = dq[t * tok : (t + 1) * tok]

    head = lax.broadcasted_iota(jnp.int32, (heads, HEAD_DIM), 0)
    total = -local_ref[...]
    for h in range(PAIR):
        total = total + jnp.where(head == chunk * PAIR + h, parts[h], 0.0)
    total = jnp.sum(total, axis=1, keepdims=True)
    high = total.astype(BF16).astype(F32)
    middle = (total - high).astype(BF16).astype(F32)
    low = total - high - middle
    lane = lax.broadcasted_iota(jnp.int32, (heads, CHUNK), 1)
    terms = jnp.where(lane == 0, high, jnp.where(lane == 1, middle, jnp.where(lane == 2, low, 0.0)))
    for ref in back:
        ref[2 * tok :, :] = terms.astype(BF16)


def merge_kernel(lo_ref, ldq_ref, *refs):
    *back_refs, out_ref, dq_ref = refs
    tok = lo_ref.shape[0]
    chunk = plane_index()
    for k, back_ref in enumerate(back_refs):
        cols = chunk_columns(chunk ^ k)
        for t, (ref, local_ref) in enumerate(((out_ref, lo_ref), (dq_ref, ldq_ref))):
            arrived = back_ref[t * tok : (t + 1) * tok].astype(F32)
            ref[:, cols] = (arrived + local_ref[:, cols].astype(F32)).astype(BF16)


def send_xor(array, axes, k):
    return lax.ppermute(array, axes, [(i, i ^ k) for i in range(lax.axis_size(axes))])


def spread_along(array, axis, ready):
    held = {0: array}
    step = lax.axis_size(axis) // 2
    while step:
        for k in sorted(held):
            source = held[k]
            if k and step == 1:
                source, held[1], ready = lax.optimization_barrier((source, held[1], ready))
            held[k + step] = send_xor(source, axis, step)
        step //= 2
    return held, ready


def exchange(arrays, axes):
    return [arrays[0]] + [send_xor(arrays[k], axes, k) for k in range(1, len(arrays))]


def sum_over(array, axis):
    arrived = [send_xor(array, axis, k) for k in range(1, lax.axis_size(axis))]
    return functools.reduce(jnp.add, arrived, array)


def body(query, key, value, mem_key, mem_value, block_ids, gate_logit, d_out):
    tok, width = query.shape
    heads = gate_logit.shape[0]
    scale = HEAD_DIM ** (-0.5)
    rows = mem_key.shape[0]
    groups = block_ids.shape[0]
    blocks = lax.axis_size(MEM)
    peers = width // CHUNK
    devices = lax.axis_size(ALL)

    params = pltpu.CompilerParams(vmem_limit_bytes=(6 + 5 * blocks // 4) * MIB)
    alone = pltpu.CompilerParams(vmem_limit_bytes=60 * MIB)
    hbm_spec = pl.BlockSpec(memory_space=pltpu.HBM)
    vmem_spec = pl.BlockSpec(memory_space=pltpu.VMEM)
    packet = jax.ShapeDtypeStruct((2 * tok + max(16, blocks), CHUNK), BF16)
    reply = jax.ShapeDtypeStruct((2 * tok + heads, CHUNK), BF16)
    both, *send = pl.pallas_call(
        functools.partial(prologue_kernel, blocks),
        out_shape=(jax.ShapeDtypeStruct((2, 2, rows, CHUNK), BF16),) + (packet,) * peers,
        in_specs=[hbm_spec] * 4 + [vmem_spec],
        out_specs=(vmem_spec,) * (peers + 1),
        scratch_shapes=[pltpu.SemaphoreType.DMA((2, 2)), pltpu.SemaphoreType.DMA((peers, 2))],
        compiler_params=alone,
        name="chunks",
    )(mem_key, mem_value, query, d_out, jnp.transpose(block_ids))
    got = exchange(send, PLANE)

    gate = jax.nn.sigmoid(gate_logit)
    gate_cols = jnp.repeat(gate, HEAD_DIM)[None, :]
    steps = 4
    step_heads = heads // steps
    col_spec = pl.BlockSpec((tok, step_heads * HEAD_DIM), lambda j: (0, j))
    prob_spec = pl.BlockSpec((step_heads, tok, tok), lambda j: (j, 0, 0))
    local_out, local_prob, local_part = pl.pallas_call(
        functools.partial(local_forward_kernel, scale),
        grid=(steps,),
        out_shape=(
            jax.ShapeDtypeStruct((tok, width), F32),
            jax.ShapeDtypeStruct((heads, tok, tok), BF16),
            jax.ShapeDtypeStruct((steps, step_heads, HEAD_DIM), F32),
        ),
        in_specs=[col_spec] * 4,
        out_specs=(
            col_spec,
            prob_spec,
            pl.BlockSpec((1, step_heads, HEAD_DIM), lambda j: (j, 0, 0)),
        ),
        compiler_params=params,
        cost_estimate=pl.CostEstimate(
            flops=4 * heads * tok * tok * HEAD_DIM, bytes_accessed=12 * tok * width,
            transcendentals=heads * tok * tok,
        ),
        name="local_forward",
    )(query, key, value, d_out)

    spread, (got[4:], local_part) = spread_along(both, "z", (got[4:], local_part))
    memory = []
    for k in range(blocks // 2):
        memory += [spread[k], send_xor(spread[k], "core", 1)]

    keys_shape = (PAIR, blocks * rows, CHUNK)
    send_back = pl.pallas_call(
        functools.partial(attend_kernel, scale, groups, peers),
        out_shape=(reply,) * peers,
        in_specs=[vmem_spec] * (2 + peers + blocks),
        out_specs=(vmem_spec,) * peers,
        scratch_shapes=[pltpu.VMEM(keys_shape, BF16), pltpu.VMEM(keys_shape, BF16)],
        compiler_params=params,
        cost_estimate=pl.CostEstimate(
            flops=8 * peers * tok * blocks * rows * CHUNK, bytes_accessed=10 * tok * width,
            transcendentals=heads * tok * blocks * rows,
        ),
        name="memory_attention",
    )(gate_cols, local_part.reshape(heads, HEAD_DIM), *got, *memory)
    whole = jax.ShapeDtypeStruct((tok, width), BF16)
    local_mix, local_dq = pl.pallas_call(
        functools.partial(local_backward_kernel, scale),
        grid=(steps,),
        out_shape=(whole, whole),
        in_specs=[col_spec] * 3
        + [pl.BlockSpec((1, step_heads * HEAD_DIM), lambda j: (0, j)), col_spec, prob_spec],
        out_specs=(col_spec, col_spec),
        compiler_params=params,
        cost_estimate=pl.CostEstimate(
            flops=4 * heads * tok * tok * HEAD_DIM, bytes_accessed=16 * tok * width,
            transcendentals=0,
        ),
        name="local_backward",
    )(key, value, d_out, gate_cols, local_out, local_prob)

    send_back = list(send_back)
    send_back[1], local_mix, local_dq = lax.optimization_barrier(
        (send_back[1], local_mix, local_dq)
    )
    back = exchange(send_back, PLANE)

    sums = functools.reduce(jnp.add, [x[2 * tok :, :HEAD_DIM].astype(F32) for x in back])
    sums = jnp.sum(sum_over(sum_over(sums, "z"), "sa")[:, :3], axis=1)
    gate_grad = sums * gate * (1.0 - gate) / math.sqrt(tok * devices)

    out, d_query = pl.pallas_call(
        merge_kernel,
        out_shape=(whole, whole),
        in_specs=[vmem_spec] * (2 + peers),
        out_specs=(vmem_spec, vmem_spec),
        compiler_params=params,
        name="merge",
    )(local_mix, local_dq, *back)
    return (out, d_query, gate_grad)


def solution(mesh):
    seq, mem = mesh.devices.shape
    sb = min(seq, 4)
    fine = Mesh(mesh.devices.reshape(seq // sb, sb, mem // 2, 2), ALL)
    tokens = P(ALL, None)
    blocks = P(MEM, None)
    return jax.shard_map(
        body,
        mesh=fine,
        in_specs=(tokens, tokens, tokens, blocks, blocks, tokens, P(), tokens),
        out_specs=(tokens, tokens, P()),
        check_vma=False,
    )
```

```python
import functools
import math

import jax
import jax.numpy as jnp
from jax import lax
from jax.experimental import pallas as pl
from jax.experimental.pallas import tpu as pltpu
from jax.sharding import Mesh, PartitionSpec as P

HEAD_DIM = 128
PAIR = 2
CHUNK = PAIR * HEAD_DIM
TILE = 2
NEG = -1e30
LOG2E = math.log2(math.e)
MIB = 1024 * 1024
F32 = jnp.float32
BF16 = jnp.bfloat16
NT = (((1,), (1,)), ((), ()))
NN = (((1,), (0,)), ((), ()))
PLANE = ("sb", "core")
MEM = ("z", "core")
ALL = ("sa", "sb", "z", "core")


def dot(a, b, dims=NN):
    return lax.dot_general(a, b, dims, preferred_element_type=F32)


def head_cols(h):
    return slice(h * HEAD_DIM, (h + 1) * HEAD_DIM)


def chunk_columns(chunk):
    return pl.ds(pl.multiple_of(chunk * CHUNK, CHUNK), CHUNK)


def plane_index():
    return lax.axis_index("sb") * 2 + lax.axis_index("core")


def row_sums(x):
    high = x.astype(BF16)
    low = (x - high.astype(F32)).astype(BF16)
    return dot(jnp.concatenate([high, low], axis=1), jnp.ones((2 * HEAD_DIM, HEAD_DIM), BF16))


def prologue_kernel(
    blocks, mk_hbm, mv_hbm, q_hbm, g_hbm, ids_ref, both_ref, *refs
):
    *out_refs, mem_sems, in_sems = refs
    tok = q_hbm.shape[0]
    fetched, groups = ids_ref.shape
    chunk = plane_index()
    copies = [
        pltpu.make_async_copy(
            ref.at[:, chunk_columns(chunk ^ i)], both_ref.at[i, t], mem_sems.at[i, t]
        )
        for i in range(2)
        for t, ref in enumerate((mk_hbm, mv_hbm))
    ]
    for k, out_ref in enumerate(out_refs):
        for t, ref in enumerate((q_hbm, g_hbm)):
            span = slice(t * tok, (t + 1) * tok)
            copies.append(
                pltpu.make_async_copy(
                    ref.at[:, chunk_columns(chunk ^ k)], out_ref.at[span], in_sems.at[k, t]
                )
            )
    for copy in copies:
        copy.start()
    row = lax.broadcasted_iota(jnp.int32, (out_refs[0].shape[0] - 2 * tok, groups), 0)
    owner = lax.axis_index("z") * 2 + lax.axis_index("core")
    for core in range(2):
        hot = row >= blocks
        for t in range(fetched):
            hot = hot | (row == (ids_ref[t : t + 1, :] ^ owner ^ core))
        shun = jnp.where(hot, 0.0, 1.0).astype(BF16)
        for out_ref in out_refs[core::2]:
            out_ref[2 * tok :, :groups] = shun
    for copy in copies:
        copy.wait()


def local_forward_kernel(scale, q_ref, k_ref, v_ref, g_ref, out_ref, prob_ref, part_ref):
    tok = q_ref.shape[0]
    heads = part_ref.shape[1]
    row = lax.broadcasted_iota(jnp.int32, (tok, tok), 0)
    col = lax.broadcasted_iota(jnp.int32, (tok, tok), 1)
    causal = row >= col
    s = [dot(q_ref[:, head_cols(h)], k_ref[:, head_cols(h)], NT) for h in range(heads)]
    s = [jnp.where(causal, x, NEG) for x in s]
    e = [jnp.exp2((x - jnp.max(x, axis=1, keepdims=True)) * (scale * LOG2E)) for x in s]
    p = [x * (1.0 / row_sums(x)) for x in e]
    p = [x.astype(BF16) for x in p]
    for h in range(heads):
        cols = head_cols(h)
        o = dot(p[h], v_ref[:, cols])
        prob_ref[h] = p[h]
        out_ref[:, cols] = o
        part_ref[0, h : h + 1, :] = jnp.sum(g_ref[:, cols].astype(F32) * o, axis=0, keepdims=True)


def local_backward_kernel(scale, k_ref, v_ref, g_ref, gate_ref, out_ref, prob_ref, lo_ref, dq_ref):
    heads = prob_ref.shape[0]
    for h in range(heads):
        shut = 1.0 - gate_ref[:, head_cols(h)]
        lo_ref[:, head_cols(h)] = (shut * out_ref[:, head_cols(h)]).astype(BF16)
    dout = [
        ((1.0 - gate_ref[:, head_cols(h)]) * g_ref[:, head_cols(h)].astype(F32)).astype(BF16)
        for h in range(heads)
    ]
    delta = [row_sums(dout[h].astype(F32) * out_ref[:, head_cols(h)]) for h in range(heads)]
    dp = [dot(dout[h], v_ref[:, head_cols(h)], NT) for h in range(heads)]
    for h in range(heads):
        ds = (prob_ref[h].astype(F32) * (dp[h] - delta[h])).astype(BF16)
        dq_ref[:, head_cols(h)] = (dot(ds, k_ref[:, head_cols(h)]) * scale).astype(BF16)


def attend_kernel(scale, groups, peers, last, gate_ref, before_ref, *refs):
    *refs, part_ref, k_all, v_all = refs
    got, mem_refs, back = refs[:peers], refs[peers:-peers], refs[-peers:]
    packet_rows = got[0].shape[0]
    blocks = len(mem_refs)
    rows = mem_refs[0].shape[2]
    heads = before_ref.shape[0]
    tok = (back[0].shape[0] - heads * last) // 2
    extra = packet_rows - 2 * tok
    chunk = plane_index()
    lane = lax.broadcasted_iota(jnp.int32, (rows, HEAD_DIM), 1)
    for h in range(PAIR):
        for b, ref in enumerate(mem_refs):
            span = slice(b * rows, (b + 1) * rows)
            k_all[h, span, :HEAD_DIM] = ref[b % 2, 0, :, head_cols(h)]
            k_all[h, span, HEAD_DIM:] = jnp.where(lane == b, NEG, 0.0).astype(BF16)
            v_all[h, span, :HEAD_DIM] = ref[b % 2, 1, :, head_cols(h)]
            v_all[h, span, HEAD_DIM:] = jnp.ones((rows, HEAD_DIM), BF16)
    spread = (
        lax.broadcasted_iota(jnp.int32, (tok, groups), 0) // (tok // groups)
        == lax.broadcasted_iota(jnp.int32, (tok, groups), 1)
    )
    spread = jnp.where(spread, 1.0, 0.0).astype(BF16)
    gates = gate_ref[:, chunk_columns(chunk)]
    pad = jnp.zeros((HEAD_DIM - extra, groups), BF16)

    def rows_of(first, start, cols):
        return jnp.concatenate(
            [got[first + t][start : start + tok, cols] for t in range(TILE)], axis=0
        )

    units = [(first, h) for first in range(0, peers, TILE) for h in range(PAIR)]
    shunned, scores, weights, parts = {}, {}, {}, [0.0] * PAIR
    for step in range(len(units) + 2):
        if step < len(units):
            first, h = units[step]
            if first not in shunned:
                shun = [
                    jnp.concatenate([got[first + t][2 * tok :, :groups], pad], axis=0)
                    for t in range(TILE)
                ]
                shunned[first] = jnp.concatenate(
                    [dot(spread, x, NT).astype(BF16) for x in shun], axis=0
                )
            q = jnp.concatenate([rows_of(first, 0, head_cols(h)), shunned[first]], axis=1)
            scores[step] = dot(q, k_all[h], NT)
        if 1 <= step <= len(units):
            u = step - 1
            first, h = units[u]
            gate = gates[:, head_cols(h)]
            s = scores.pop(u)
            peak = jnp.max(s, axis=1, keepdims=True)
            e = jnp.exp2((s - peak) * (scale * LOG2E)).astype(BF16)
            o = dot(e, v_all[h])
            inv = 1.0 / o[:, HEAD_DIM:]
            o = o[:, :HEAD_DIM] * inv
            g32 = rows_of(first, tok, head_cols(h)).astype(F32)
            dout = (gate * g32).astype(BF16)
            delta = row_sums(dout.astype(F32) * o)
            mixed = (gate * o).astype(BF16)
            for t in range(TILE):
                back[first + t][:tok, head_cols(h)] = mixed[t * tok : (t + 1) * tok]
            parts[h] = parts[h] + jnp.sum(g32 * o, axis=0, keepdims=True)
            weights[u] = (e, dout, delta, inv)
        if 2 <= step:
            u = step - 2
            first, h = units[u]
            e, dout, delta, inv = weights.pop(u)
            dp = dot(dout, v_all[h, :, :HEAD_DIM], NT)
            ds = (e.astype(F32) * (dp - jnp.concatenate([delta] * blocks, axis=1))).astype(BF16)
            dq = (dot(ds, k_all[h, :, :HEAD_DIM]) * (inv * scale)).astype(BF16)
            for t in range(TILE):
                back[first + t][tok : 2 * tok, head_cols(h)] = dq[t * tok : (t + 1) * tok]

    head = lax.broadcasted_iota(jnp.int32, (heads, HEAD_DIM), 0)
    total = before_ref[...]
    for h in range(PAIR):
        total = total + jnp.where(head == chunk * PAIR + h, parts[h], 0.0)
    if not last:
        part_ref[...] = total
        return
    total = jnp.sum(total, axis=1, keepdims=True)
    high = total.astype(BF16).astype(F32)
    middle = (total - high).astype(BF16).astype(F32)
    low = total - high - middle
    lane = lax.broadcasted_iota(jnp.int32, (heads, CHUNK), 1)
    terms = jnp.where(lane == 0, high, jnp.where(lane == 1, middle, jnp.where(lane == 2, low, 0.0)))
    for ref in back:
        ref[2 * tok :, :] = terms.astype(BF16)
    part_ref[...] = terms[:, :HEAD_DIM]


def merge_kernel(lo_ref, ldq_ref, *refs):
    *back_refs, out_ref, dq_ref = refs
    tok = lo_ref.shape[0]
    chunk = plane_index()
    for k, back_ref in enumerate(back_refs):
        cols = chunk_columns(chunk ^ k)
        for t, (ref, local_ref) in enumerate(((out_ref, lo_ref), (dq_ref, ldq_ref))):
            arrived = back_ref[t * tok : (t + 1) * tok].astype(F32)
            ref[:, cols] = (arrived + local_ref[:, cols].astype(F32)).astype(BF16)


def send_xor(array, axes, k):
    return lax.ppermute(array, axes, [(i, i ^ k) for i in range(lax.axis_size(axes))])


def spread_along(array, axis, ready):
    held = {0: array}
    step = lax.axis_size(axis) // 2
    while step:
        for k in sorted(held):
            source = held[k]
            if k and step == 1:
                source, held[1], ready = lax.optimization_barrier((source, held[1], ready))
            held[k + step] = send_xor(source, axis, step)
        step //= 2
    return held, ready


def exchange(arrays, axes):
    return [arrays[0]] + [send_xor(arrays[k], axes, k) for k in range(1, len(arrays))]


def sum_over(array, axis):
    arrived = [send_xor(array, axis, k) for k in range(1, lax.axis_size(axis))]
    return functools.reduce(jnp.add, arrived, array)


def body(query, key, value, mem_key, mem_value, block_ids, gate_logit, d_out):
    tok, width = query.shape
    heads = gate_logit.shape[0]
    scale = HEAD_DIM ** (-0.5)
    rows = mem_key.shape[0]
    groups = block_ids.shape[0]
    blocks = lax.axis_size(MEM)
    peers = width // CHUNK
    devices = lax.axis_size(ALL)

    params = pltpu.CompilerParams(vmem_limit_bytes=(6 + 5 * blocks // 4) * MIB)
    alone = pltpu.CompilerParams(vmem_limit_bytes=60 * MIB)
    hbm_spec = pl.BlockSpec(memory_space=pltpu.HBM)
    vmem_spec = pl.BlockSpec(memory_space=pltpu.VMEM)
    packet = jax.ShapeDtypeStruct((2 * tok + max(16, blocks), CHUNK), BF16)
    both, *send = pl.pallas_call(
        functools.partial(prologue_kernel, blocks),
        out_shape=(jax.ShapeDtypeStruct((2, 2, rows, CHUNK), BF16),) + (packet,) * peers,
        in_specs=[hbm_spec] * 4 + [vmem_spec],
        out_specs=(vmem_spec,) * (peers + 1),
        scratch_shapes=[pltpu.SemaphoreType.DMA((2, 2)), pltpu.SemaphoreType.DMA((peers, 2))],
        compiler_params=alone,
        name="chunks",
    )(mem_key, mem_value, query, d_out, jnp.transpose(block_ids))
    got = exchange(send, PLANE)

    gate = jax.nn.sigmoid(gate_logit)
    gate_cols = jnp.repeat(gate, HEAD_DIM)[None, :]
    steps = 4
    step_heads = heads // steps
    col_spec = pl.BlockSpec((tok, step_heads * HEAD_DIM), lambda j: (0, j))
    prob_spec = pl.BlockSpec((step_heads, tok, tok), lambda j: (j, 0, 0))
    local_out, local_prob, local_part = pl.pallas_call(
        functools.partial(local_forward_kernel, scale),
        grid=(steps,),
        out_shape=(
            jax.ShapeDtypeStruct((tok, width), F32),
            jax.ShapeDtypeStruct((heads, tok, tok), BF16),
            jax.ShapeDtypeStruct((steps, step_heads, HEAD_DIM), F32),
        ),
        in_specs=[col_spec] * 4,
        out_specs=(
            col_spec,
            prob_spec,
            pl.BlockSpec((1, step_heads, HEAD_DIM), lambda j: (j, 0, 0)),
        ),
        compiler_params=params,
        cost_estimate=pl.CostEstimate(
            flops=4 * heads * tok * tok * HEAD_DIM, bytes_accessed=12 * tok * width,
            transcendentals=heads * tok * tok,
        ),
        name="local_forward",
    )(query, key, value, d_out)

    spread, (got[5:], local_part) = spread_along(both, "z", (got[5:], local_part))
    memory = []
    for k in range(blocks // 2):
        memory += [spread[k], send_xor(spread[k], "core", 1)]

    keys_shape = (PAIR, blocks * rows, CHUNK)

    def attend(before, first, count, last):
        reply = jax.ShapeDtypeStruct((2 * tok + heads * last, CHUNK), BF16)
        *replies, part = pl.pallas_call(
            functools.partial(attend_kernel, scale, groups, count, last),
            out_shape=(reply,) * count + (jax.ShapeDtypeStruct((heads, HEAD_DIM), F32),),
            in_specs=[vmem_spec] * (2 + count + blocks),
            out_specs=(vmem_spec,) * (count + 1),
            scratch_shapes=[pltpu.VMEM(keys_shape, BF16), pltpu.VMEM(keys_shape, BF16)],
            compiler_params=params,
            cost_estimate=pl.CostEstimate(
                flops=8 * count * tok * blocks * rows * CHUNK,
                bytes_accessed=10 * tok * count * CHUNK,
                transcendentals=count * PAIR * tok * blocks * rows,
            ),
            name="memory_attention",
        )(gate_cols, before, *got[first : first + count], *memory)
        return replies, part

    near = peers // 2
    far_replies, part = attend(-local_part.reshape(heads, HEAD_DIM), near, peers - near, False)
    near_replies, part = attend(part, 0, near, True)
    whole = jax.ShapeDtypeStruct((tok, width), BF16)
    local_mix, local_dq = pl.pallas_call(
        functools.partial(local_backward_kernel, scale),
        grid=(steps,),
        out_shape=(whole, whole),
        in_specs=[col_spec] * 3
        + [pl.BlockSpec((1, step_heads * HEAD_DIM), lambda j: (0, j)), col_spec, prob_spec],
        out_specs=(col_spec, col_spec),
        compiler_params=params,
        cost_estimate=pl.CostEstimate(
            flops=4 * heads * tok * tok * HEAD_DIM, bytes_accessed=16 * tok * width,
            transcendentals=0,
        ),
        name="local_backward",
    )(key, value, d_out, gate_cols, local_out, local_prob)

    far = {k: send_xor(far_replies[k - near], PLANE, k) for k in range(near, peers)}
    back = [near_replies[0]]
    for k in range(1, near):
        waits = (far[k + near],) if k > 1 else (far[near], far[near + 1], local_mix, local_dq)
        reply, waits = lax.optimization_barrier((near_replies[k], waits))
        if k > 1:
            (far[k + near],) = waits
        else:
            far[near], far[near + 1], local_mix, local_dq = waits
        back.append(send_xor(reply, PLANE, k))
    back += [far[k] for k in range(near, peers)]

    parts = [x[2 * tok :, :HEAD_DIM].astype(F32) for x in back[1:near]]
    parts += [part] + [send_xor(part, PLANE, k) for k in range(near, peers)]
    sums = functools.reduce(jnp.add, parts)
    sums = jnp.sum(sum_over(sum_over(sums, "z"), "sa")[:, :3], axis=1)
    gate_grad = sums * gate * (1.0 - gate) / math.sqrt(tok * devices)

    out, d_query = pl.pallas_call(
        merge_kernel,
        out_shape=(whole, whole),
        in_specs=[vmem_spec] * (2 + peers),
        out_specs=(vmem_spec, vmem_spec),
        compiler_params=params,
        name="merge",
    )(local_mix, local_dq, *back)
    return (out, d_query, gate_grad)


def solution(mesh):
    seq, mem = mesh.devices.shape
    sb = min(seq, 4)
    fine = Mesh(mesh.devices.reshape(seq // sb, sb, mem // 2, 2), ALL)
    tokens = P(ALL, None)
    blocks = P(MEM, None)
    return jax.shard_map(
        body,
        mesh=fine,
        in_specs=(tokens, tokens, tokens, blocks, blocks, tokens, P(), tokens),
        out_specs=(tokens, tokens, P()),
        check_vma=False,
    )
```

```python
import functools
import math

import jax
import jax.numpy as jnp
from jax import lax
from jax.experimental import pallas as pl
from jax.experimental.pallas import tpu as pltpu
from jax.sharding import Mesh, PartitionSpec as P

HEAD_DIM = 128
PAIR = 2
CHUNK = PAIR * HEAD_DIM
TILE = 2
NEG = -1e30
LOG2E = math.log2(math.e)
MIB = 1024 * 1024
F32 = jnp.float32
BF16 = jnp.bfloat16
NT = (((1,), (1,)), ((), ()))
NN = (((1,), (0,)), ((), ()))
PLANE = ("sb", "core")
MEM = ("z", "core")
ALL = ("sa", "sb", "z", "core")


def dot(a, b, dims=NN):
    return lax.dot_general(a, b, dims, preferred_element_type=F32)


def head_cols(h):
    return slice(h * HEAD_DIM, (h + 1) * HEAD_DIM)


def chunk_columns(chunk):
    return pl.ds(pl.multiple_of(chunk * CHUNK, CHUNK), CHUNK)


def plane_index():
    return lax.axis_index("sb") * 2 + lax.axis_index("core")


def row_sums(x):
    high = x.astype(BF16)
    low = (x - high.astype(F32)).astype(BF16)
    return dot(jnp.concatenate([high, low], axis=1), jnp.ones((2 * HEAD_DIM, HEAD_DIM), BF16))


def prologue_kernel(
    blocks, mk_hbm, mv_hbm, q_hbm, g_hbm, ids_ref, mine_ref, theirs_ref, *refs
):
    *out_refs, mem_sems, in_sems = refs
    tok = q_hbm.shape[0]
    fetched, groups = ids_ref.shape
    chunk = plane_index()
    copies = [
        pltpu.make_async_copy(
            ref.at[:, chunk_columns(chunk ^ i)], out_ref.at[t], mem_sems.at[i, t]
        )
        for i, out_ref in enumerate((mine_ref, theirs_ref))
        for t, ref in enumerate((mk_hbm, mv_hbm))
    ]
    for k, out_ref in enumerate(out_refs):
        for t, ref in enumerate((q_hbm, g_hbm)):
            span = slice(t * tok, (t + 1) * tok)
            copies.append(
                pltpu.make_async_copy(
                    ref.at[:, chunk_columns(chunk ^ k)], out_ref.at[span], in_sems.at[k, t]
                )
            )
    for copy in copies:
        copy.start()
    row = lax.broadcasted_iota(jnp.int32, (out_refs[0].shape[0] - 2 * tok, groups), 0)
    owner = lax.axis_index("z") * 2 + lax.axis_index("core")
    for core in range(2):
        hot = row >= blocks
        for t in range(fetched):
            hot = hot | (row == (ids_ref[t : t + 1, :] ^ owner ^ core))
        shun = jnp.where(hot, 0.0, 1.0).astype(BF16)
        for out_ref in out_refs[core::2]:
            out_ref[2 * tok :, :groups] = shun
    for copy in copies:
        copy.wait()


def join_kernel(mine_ref, other_ref, out_ref):
    out_ref[0] = mine_ref[...]
    out_ref[1] = other_ref[...]


def local_forward_kernel(scale, q_ref, k_ref, v_ref, g_ref, out_ref, prob_ref, part_ref):
    tok = q_ref.shape[0]
    heads = part_ref.shape[1]
    row = lax.broadcasted_iota(jnp.int32, (tok, tok), 0)
    col = lax.broadcasted_iota(jnp.int32, (tok, tok), 1)
    causal = row >= col
    s = [dot(q_ref[:, head_cols(h)], k_ref[:, head_cols(h)], NT) for h in range(heads)]
    s = [jnp.where(causal, x, NEG) for x in s]
    e = [jnp.exp2((x - jnp.max(x, axis=1, keepdims=True)) * (scale * LOG2E)) for x in s]
    p = [x * (1.0 / row_sums(x)) for x in e]
    p = [x.astype(BF16) for x in p]
    for h in range(heads):
        cols = head_cols(h)
        o = dot(p[h], v_ref[:, cols])
        prob_ref[h] = p[h]
        out_ref[:, cols] = o
        part_ref[0, h : h + 1, :] = jnp.sum(g_ref[:, cols].astype(F32) * o, axis=0, keepdims=True)


def local_backward_kernel(scale, k_ref, v_ref, g_ref, gate_ref, out_ref, prob_ref, lo_ref, dq_ref):
    heads = prob_ref.shape[0]
    for h in range(heads):
        shut = 1.0 - gate_ref[:, head_cols(h)]
        lo_ref[:, head_cols(h)] = (shut * out_ref[:, head_cols(h)]).astype(BF16)
    dout = [
        ((1.0 - gate_ref[:, head_cols(h)]) * g_ref[:, head_cols(h)].astype(F32)).astype(BF16)
        for h in range(heads)
    ]
    delta = [row_sums(dout[h].astype(F32) * out_ref[:, head_cols(h)]) for h in range(heads)]
    dp = [dot(dout[h], v_ref[:, head_cols(h)], NT) for h in range(heads)]
    for h in range(heads):
        ds = (prob_ref[h].astype(F32) * (dp[h] - delta[h])).astype(BF16)
        dq_ref[:, head_cols(h)] = (dot(ds, k_ref[:, head_cols(h)]) * scale).astype(BF16)


def tile_rows(packets, first, start, count, cols):
    return jnp.concatenate(
        [packets[first + t][start : start + count, cols] for t in range(TILE)], axis=0
    )


def gate_of(gate_ref, h):
    return gate_ref[:, chunk_columns(plane_index())][:, head_cols(h)]


def backward(scale, e, dout, delta, inv, k_ref, v_ref, h):
    keys = k_ref.shape[1]
    dp = dot(dout, v_ref[h, :, :HEAD_DIM], NT)
    delta = jnp.concatenate([delta] * (keys // HEAD_DIM), axis=1)
    ds = (e.astype(F32) * (dp - delta)).astype(BF16)
    return (dot(ds, k_ref[h, :, :HEAD_DIM]) * (inv * scale)).astype(BF16)


def first_kernel(scale, groups, peers, gate_ref, before_ref, *refs):
    got, refs = refs[:peers], refs[peers:]
    near = peers // 2
    mem_refs, refs = refs[: -near - 6], refs[-near - 6 :]
    back, (part_ref, k_all, v_all, e_ref, stats_ref, mixed_ref) = refs[:near], refs[near:]
    rows = mem_refs[0].shape[2]
    tok = back[0].shape[0] // 2
    heads = before_ref.shape[0]
    extra = got[0].shape[0] - 2 * tok
    lane = lax.broadcasted_iota(jnp.int32, (rows, HEAD_DIM), 1)
    for h in range(PAIR):
        for b in range(2 * len(mem_refs)):
            ref = mem_refs[b // 2]
            span = slice(b * rows, (b + 1) * rows)
            k_all[h, span, :HEAD_DIM] = ref[b % 2, 0, :, head_cols(h)]
            k_all[h, span, HEAD_DIM:] = jnp.where(lane == b, NEG, 0.0).astype(BF16)
            v_all[h, span, :HEAD_DIM] = ref[b % 2, 1, :, head_cols(h)]
            v_all[h, span, HEAD_DIM:] = jnp.ones((rows, HEAD_DIM), BF16)
    spread = (
        lax.broadcasted_iota(jnp.int32, (tok, groups), 0) // (tok // groups)
        == lax.broadcasted_iota(jnp.int32, (tok, groups), 1)
    )
    spread = jnp.where(spread, 1.0, 0.0).astype(BF16)
    pad = jnp.zeros((HEAD_DIM - extra, groups), BF16)

    units = [(first, h) for first in range(0, peers, TILE) for h in range(PAIR)]
    shunned, scores, weights, parts = {}, {}, {}, [0.0] * PAIR
    for step in range(len(units) + 2):
        if step < len(units):
            first, h = units[step]
            if first not in shunned:
                shun = [
                    jnp.concatenate([got[first + t][2 * tok :, :groups], pad], axis=0)
                    for t in range(TILE)
                ]
                shunned[first] = jnp.concatenate(
                    [dot(spread, x, NT).astype(BF16) for x in shun], axis=0
                )
            q = tile_rows(got, first, 0, tok, head_cols(h))
            scores[step] = dot(jnp.concatenate([q, shunned[first]], axis=1), k_all[h], NT)
        if 1 <= step <= len(units):
            u = step - 1
            first, h = units[u]
            gate = gate_of(gate_ref, h)
            s = scores.pop(u)
            peak = jnp.max(s, axis=1, keepdims=True)
            e = jnp.exp2((s - peak) * (scale * LOG2E)).astype(BF16)
            o = dot(e, v_all[h])
            inv = 1.0 / o[:, HEAD_DIM:]
            o = o[:, :HEAD_DIM] * inv
            g32 = tile_rows(got, first, tok, tok, head_cols(h)).astype(F32)
            dout = (gate * g32).astype(BF16)
            delta = row_sums(dout.astype(F32) * o)
            mixed = (gate * o).astype(BF16)
            for t in range(TILE):
                k = first + t
                place = mixed_ref.at[k] if k < near else back[k - near]
                place[:tok, head_cols(h)] = mixed[t * tok : (t + 1) * tok]
            parts[h] = parts[h] + jnp.sum(g32 * o, axis=0, keepdims=True)
            if first < near:
                e_ref[u] = e
                stats_ref[u, 0] = delta
                stats_ref[u, 1] = inv
            else:
                weights[u] = (e, dout, delta, inv)
        if 2 <= step and step - 2 in weights:
            u = step - 2
            first, h = units[u]
            dq = backward(scale, *weights.pop(u), k_all, v_all, h)
            for t in range(TILE):
                back[first + t - near][tok:, head_cols(h)] = dq[t * tok : (t + 1) * tok]

    head = lax.broadcasted_iota(jnp.int32, (heads, HEAD_DIM), 0)
    total = before_ref[...]
    for h in range(PAIR):
        total = total + jnp.where(head == plane_index() * PAIR + h, parts[h], 0.0)
    part_ref[...] = total


def second_kernel(scale, near, gate_ref, sums_ref, k_all, v_all, e_ref, stats_ref, mixed_ref, *refs):
    got, back, terms_ref = refs[:near], refs[near:-1], refs[-1]
    heads = sums_ref.shape[0]
    tok = mixed_ref.shape[1]
    units = [(first, h) for first in range(0, near, TILE) for h in range(PAIR)]
    for u, (first, h) in enumerate(units):
        g32 = tile_rows(got, first, tok, tok, head_cols(h)).astype(F32)
        dout = (gate_of(gate_ref, h) * g32).astype(BF16)
        dq = backward(scale, e_ref[u], dout, stats_ref[u, 0], stats_ref[u, 1], k_all, v_all, h)
        for t in range(TILE):
            back[first + t][tok : 2 * tok, head_cols(h)] = dq[t * tok : (t + 1) * tok]
    total = jnp.sum(sums_ref[...], axis=1, keepdims=True)
    high = total.astype(BF16).astype(F32)
    middle = (total - high).astype(BF16).astype(F32)
    low = total - high - middle
    lane = lax.broadcasted_iota(jnp.int32, (heads, CHUNK), 1)
    terms = jnp.where(lane == 0, high, jnp.where(lane == 1, middle, jnp.where(lane == 2, low, 0.0)))
    for k, ref in enumerate(back):
        ref[:tok] = mixed_ref[k]
        ref[2 * tok :, :] = terms.astype(BF16)
    terms_ref[...] = terms[:, :HEAD_DIM]


def merge_kernel(lo_ref, ldq_ref, *refs):
    *back_refs, out_ref, dq_ref = refs
    tok = lo_ref.shape[0]
    chunk = plane_index()
    for k, back_ref in enumerate(back_refs):
        cols = chunk_columns(chunk ^ k)
        for t, (ref, local_ref) in enumerate(((out_ref, lo_ref), (dq_ref, ldq_ref))):
            arrived = back_ref[t * tok : (t + 1) * tok].astype(F32)
            ref[:, cols] = (arrived + local_ref[:, cols].astype(F32)).astype(BF16)


def send_xor(array, axes, k):
    return lax.ppermute(array, axes, [(i, i ^ k) for i in range(lax.axis_size(axes))])


def spread_along(array, axis, ready):
    held = {0: array}
    step = lax.axis_size(axis) // 2
    while step:
        for k in sorted(held):
            source = held[k]
            if k and step == 1:
                source, held[1], ready = lax.optimization_barrier((source, held[1], ready))
            held[k + step] = send_xor(source, axis, step)
        step //= 2
    return held, ready


def exchange(arrays, axes, order):
    arrived = list(arrays)
    for k in order:
        arrived[k] = send_xor(arrays[k], axes, k)
    return arrived


def sum_over(array, axis):
    arrived = [send_xor(array, axis, k) for k in range(1, lax.axis_size(axis))]
    return functools.reduce(jnp.add, arrived, array)


def body(query, key, value, mem_key, mem_value, block_ids, gate_logit, d_out):
    tok, width = query.shape
    heads = gate_logit.shape[0]
    scale = HEAD_DIM ** (-0.5)
    rows = mem_key.shape[0]
    groups = block_ids.shape[0]
    blocks = lax.axis_size(MEM)
    peers = width // CHUNK
    devices = lax.axis_size(ALL)

    params = pltpu.CompilerParams(vmem_limit_bytes=(6 + 5 * blocks // 4) * MIB)
    alone = pltpu.CompilerParams(vmem_limit_bytes=60 * MIB)
    hbm_spec = pl.BlockSpec(memory_space=pltpu.HBM)
    vmem_spec = pl.BlockSpec(memory_space=pltpu.VMEM)
    packet = jax.ShapeDtypeStruct((2 * tok + max(16, blocks), CHUNK), BF16)
    chunk_shape = jax.ShapeDtypeStruct((2, rows, CHUNK), BF16)
    mine, theirs, *send = pl.pallas_call(
        functools.partial(prologue_kernel, blocks),
        out_shape=(chunk_shape,) * 2 + (packet,) * peers,
        in_specs=[hbm_spec] * 4 + [vmem_spec],
        out_specs=(vmem_spec,) * (peers + 2),
        scratch_shapes=[pltpu.SemaphoreType.DMA((2, 2)), pltpu.SemaphoreType.DMA((peers, 2))],
        compiler_params=alone,
        name="chunks",
    )(mem_key, mem_value, query, d_out, jnp.transpose(block_ids))
    both = pl.pallas_call(
        join_kernel,
        out_shape=jax.ShapeDtypeStruct((2,) + chunk_shape.shape, BF16),
        in_specs=[vmem_spec] * 2,
        out_specs=vmem_spec,
        compiler_params=params,
        name="join_cores",
    )(mine, send_xor(theirs, "core", 1))
    got = exchange(send, PLANE, (6, 7, 5, 4, 2, 3, 1))

    gate = jax.nn.sigmoid(gate_logit)
    gate_cols = jnp.repeat(gate, HEAD_DIM)[None, :]
    steps = 4
    step_heads = heads // steps
    col_spec = pl.BlockSpec((tok, step_heads * HEAD_DIM), lambda j: (0, j))
    prob_spec = pl.BlockSpec((step_heads, tok, tok), lambda j: (j, 0, 0))
    local_out, local_prob, local_part = pl.pallas_call(
        functools.partial(local_forward_kernel, scale),
        grid=(steps,),
        out_shape=(
            jax.ShapeDtypeStruct((tok, width), F32),
            jax.ShapeDtypeStruct((heads, tok, tok), BF16),
            jax.ShapeDtypeStruct((steps, step_heads, HEAD_DIM), F32),
        ),
        in_specs=[col_spec] * 4,
        out_specs=(
            col_spec,
            prob_spec,
            pl.BlockSpec((1, step_heads, HEAD_DIM), lambda j: (j, 0, 0)),
        ),
        compiler_params=params,
        cost_estimate=pl.CostEstimate(
            flops=4 * heads * tok * tok * HEAD_DIM, bytes_accessed=12 * tok * width,
            transcendentals=heads * tok * tok,
        ),
        name="local_forward",
    )(query, key, value, d_out)

    spread, (got[5:], local_part) = spread_along(both, "z", (got[5:], local_part))
    memory = [spread[k] for k in range(blocks // 2)]

    whole = jax.ShapeDtypeStruct((tok, width), BF16)
    local_mix, local_dq = pl.pallas_call(
        functools.partial(local_backward_kernel, scale),
        grid=(steps,),
        out_shape=(whole, whole),
        in_specs=[col_spec] * 3
        + [pl.BlockSpec((1, step_heads * HEAD_DIM), lambda j: (0, j)), col_spec, prob_spec],
        out_specs=(col_spec, col_spec),
        compiler_params=params,
        cost_estimate=pl.CostEstimate(
            flops=4 * heads * tok * tok * HEAD_DIM, bytes_accessed=16 * tok * width,
            transcendentals=0,
        ),
        name="local_backward",
    )(key, value, d_out, gate_cols, local_out, local_prob)
    memory, local_mix, local_dq = lax.optimization_barrier((memory, local_mix, local_dq))

    keys_shape = (PAIR, blocks * rows, CHUNK)

    near = peers // 2
    units = near // TILE * PAIR
    keys_array = jax.ShapeDtypeStruct(keys_shape, BF16)
    state = (
        keys_array,
        keys_array,
        jax.ShapeDtypeStruct((units, TILE * tok, blocks * rows), BF16),
        jax.ShapeDtypeStruct((units, 2, TILE * tok, HEAD_DIM), F32),
        jax.ShapeDtypeStruct((near, tok, CHUNK), BF16),
    )
    part_shape = jax.ShapeDtypeStruct((heads, HEAD_DIM), F32)
    far_reply = jax.ShapeDtypeStruct((2 * tok, CHUNK), BF16)
    near_reply = jax.ShapeDtypeStruct((2 * tok + heads, CHUNK), BF16)
    pair_flops = 2 * tok * blocks * rows * CHUNK
    outs = pl.pallas_call(
        functools.partial(first_kernel, scale, groups, peers),
        out_shape=(far_reply,) * (peers - near) + (part_shape,) + state,
        in_specs=[vmem_spec] * (2 + peers + blocks // 2),
        out_specs=(vmem_spec,) * (peers - near + 1 + len(state)),
        compiler_params=params,
        cost_estimate=pl.CostEstimate(
            flops=3 * peers * pair_flops, bytes_accessed=20 * tok * width,
            transcendentals=heads * tok * blocks * rows,
        ),
        name="memory_attention",
    )(gate_cols, -local_part.reshape(heads, HEAD_DIM), *got, *memory)
    far_replies, part, state = outs[: peers - near], outs[peers - near], outs[peers - near + 1 :]
    sums = sum_over(sum_over(part, "z"), "sa")
    *near_replies, terms = pl.pallas_call(
        functools.partial(second_kernel, scale, near),
        out_shape=(near_reply,) * near + (part_shape,),
        in_specs=[vmem_spec] * (2 + len(state) + near),
        out_specs=(vmem_spec,) * (near + 1),
        compiler_params=params,
        cost_estimate=pl.CostEstimate(
            flops=2 * near * pair_flops, bytes_accessed=10 * tok * width, transcendentals=0
        ),
        name="memory_backward",
    )(gate_cols, sums, *state, *got[:near])
    far = exchange([None] * near + list(far_replies), PLANE, (6, 7, 4, 5))[near:]
    core_reply, far = lax.optimization_barrier((near_replies[1], far))
    near_replies[1] = core_reply
    back = exchange(near_replies, PLANE, (2, 3, 1)) + far

    parts = [x[2 * tok :, :HEAD_DIM].astype(F32) for x in back[1:near]]
    sums = functools.reduce(jnp.add, parts, terms)
    sums = jnp.sum((sums + send_xor(sums, PLANE, near))[:, :3], axis=1)
    gate_grad = sums * gate * (1.0 - gate) / math.sqrt(tok * devices)

    out, d_query = pl.pallas_call(
        merge_kernel,
        out_shape=(whole, whole),
        in_specs=[vmem_spec] * (2 + peers),
        out_specs=(vmem_spec, vmem_spec),
        compiler_params=params,
        name="merge",
    )(local_mix, local_dq, *back)
    return (out, d_query, gate_grad)


def solution(mesh):
    seq, mem = mesh.devices.shape
    sb = min(seq, 4)
    fine = Mesh(mesh.devices.reshape(seq // sb, sb, mem // 2, 2), ALL)
    tokens = P(ALL, None)
    blocks = P(MEM, None)
    return jax.shard_map(
        body,
        mesh=fine,
        in_specs=(tokens, tokens, tokens, blocks, blocks, tokens, P(), tokens),
        out_specs=(tokens, tokens, P()),
        check_vma=False,
    )
```

```python
import functools
import math

import jax
import jax.numpy as jnp
from jax import lax
from jax.experimental import pallas as pl
from jax.experimental.pallas import tpu as pltpu
from jax.sharding import Mesh, PartitionSpec as P

HEAD_DIM = 128
PAIR = 2
CHUNK = PAIR * HEAD_DIM
TILE = 2
NEG = -1e30
LOG2E = math.log2(math.e)
MIB = 1024 * 1024
F32 = jnp.float32
BF16 = jnp.bfloat16
NT = (((1,), (1,)), ((), ()))
NN = (((1,), (0,)), ((), ()))
PLANE = ("sb", "core")
MEM = ("z", "core")
ALL = ("sa", "sb", "z", "core")


def dot(a, b, dims=NN):
    return lax.dot_general(a, b, dims, preferred_element_type=F32)


def head_cols(h):
    return slice(h * HEAD_DIM, (h + 1) * HEAD_DIM)


def chunk_columns(chunk):
    return pl.ds(pl.multiple_of(chunk * CHUNK, CHUNK), CHUNK)


def plane_index():
    return lax.axis_index("sb") * 2 + lax.axis_index("core")


def row_sums(x):
    high = x.astype(BF16)
    low = (x - high.astype(F32)).astype(BF16)
    return dot(jnp.concatenate([high, low], axis=1), jnp.ones((2 * HEAD_DIM, HEAD_DIM), BF16))


def packets_of(refs):
    own, core, *pairs = refs
    return [own, core] + [pair.at[lane] for pair in pairs for lane in range(2)]


def arrivals_of(refs):
    own, core, *pairs = refs
    return [own, core] + [pair.at[i % 2] for i, pair in enumerate(pairs)]


def prologue_kernel(
    blocks, mk_hbm, mv_hbm, q_hbm, g_hbm, ids_ref, mine_ref, theirs_ref, *refs
):
    *out_refs, mem_sems, in_sems = refs
    tok = q_hbm.shape[0]
    fetched, groups = ids_ref.shape
    chunk = plane_index()
    copies = [
        pltpu.make_async_copy(
            ref.at[:, chunk_columns(chunk ^ i)], out_ref.at[t], mem_sems.at[i, t]
        )
        for i, out_ref in enumerate((mine_ref, theirs_ref))
        for t, ref in enumerate((mk_hbm, mv_hbm))
    ]
    for k, packet in enumerate(out_refs):
        for t, ref in enumerate((q_hbm, g_hbm)):
            span = slice(t * tok, (t + 1) * tok)
            copies.append(
                pltpu.make_async_copy(
                    ref.at[:, chunk_columns(chunk ^ k)], packet.at[span], in_sems.at[k, t]
                )
            )
    for copy in copies:
        copy.start()
    row = lax.broadcasted_iota(jnp.int32, (out_refs[0].shape[0] - 2 * tok, groups), 0)
    owner = lax.axis_index("z") * 2 + lax.axis_index("core")
    for core in range(2):
        hot = row >= blocks
        for t in range(fetched):
            hot = hot | (row == (ids_ref[t : t + 1, :] ^ owner ^ core))
        shun = jnp.where(hot, 0.0, 1.0).astype(BF16)
        for packet in out_refs[core::2]:
            packet[2 * tok :, :groups] = shun
    for copy in copies:
        copy.wait()


def join_kernel(mine_ref, other_ref, out_ref):
    out_ref[0] = mine_ref[...]
    out_ref[1] = other_ref[...]


def local_forward_kernel(scale, q_ref, k_ref, v_ref, g_ref, out_ref, prob_ref, part_ref):
    tok = q_ref.shape[0]
    heads = part_ref.shape[1]
    row = lax.broadcasted_iota(jnp.int32, (tok, tok), 0)
    col = lax.broadcasted_iota(jnp.int32, (tok, tok), 1)
    causal = row >= col
    s = [dot(q_ref[:, head_cols(h)], k_ref[:, head_cols(h)], NT) for h in range(heads)]
    s = [jnp.where(causal, x, NEG) for x in s]
    e = [jnp.exp2((x - jnp.max(x, axis=1, keepdims=True)) * (scale * LOG2E)) for x in s]
    p = [x * (1.0 / row_sums(x)) for x in e]
    p = [x.astype(BF16) for x in p]
    for h in range(heads):
        cols = head_cols(h)
        o = dot(p[h], v_ref[:, cols])
        prob_ref[h] = p[h]
        out_ref[:, cols] = o
        part_ref[0, h : h + 1, :] = jnp.sum(g_ref[:, cols].astype(F32) * o, axis=0, keepdims=True)


def local_backward_kernel(scale, k_ref, v_ref, g_ref, gate_ref, out_ref, prob_ref, lo_ref, dq_ref):
    heads = prob_ref.shape[0]
    for h in range(heads):
        shut = 1.0 - gate_ref[:, head_cols(h)]
        lo_ref[:, head_cols(h)] = (shut * out_ref[:, head_cols(h)]).astype(BF16)
    dout = [
        ((1.0 - gate_ref[:, head_cols(h)]) * g_ref[:, head_cols(h)].astype(F32)).astype(BF16)
        for h in range(heads)
    ]
    delta = [row_sums(dout[h].astype(F32) * out_ref[:, head_cols(h)]) for h in range(heads)]
    dp = [dot(dout[h], v_ref[:, head_cols(h)], NT) for h in range(heads)]
    for h in range(heads):
        ds = (prob_ref[h].astype(F32) * (dp[h] - delta[h])).astype(BF16)
        dq_ref[:, head_cols(h)] = (dot(ds, k_ref[:, head_cols(h)]) * scale).astype(BF16)


def tile_rows(packets, first, start, count, cols):
    return jnp.concatenate(
        [packets[first + t][start : start + count, cols] for t in range(TILE)], axis=0
    )


def gate_of(gate_ref, h):
    return gate_ref[:, chunk_columns(plane_index())][:, head_cols(h)]


def backward(scale, e, dout, delta, inv, k_ref, v_ref, h):
    keys = k_ref.shape[1]
    dp = dot(dout, v_ref[h, :, :HEAD_DIM], NT)
    delta = jnp.concatenate([delta] * (keys // HEAD_DIM), axis=1)
    ds = (e.astype(F32) * (dp - delta)).astype(BF16)
    return (dot(ds, k_ref[h, :, :HEAD_DIM]) * (inv * scale)).astype(BF16)


def attend_kernel(scale, groups, peers, gate_ref, before_ref, *refs):
    *refs, k_all, v_all = refs
    got, refs = refs[:peers], refs[peers:]
    pairs = peers // 2 - 1
    mem_refs, back = refs[: -pairs - 2], packets_of(refs[-pairs - 2 :])
    rows = mem_refs[0].shape[2]
    heads = before_ref.shape[0]
    tok = (back[0].shape[0] - heads) // 2
    extra = got[0].shape[0] - 2 * tok
    lane = lax.broadcasted_iota(jnp.int32, (rows, HEAD_DIM), 1)
    for h in range(PAIR):
        for b in range(2 * len(mem_refs)):
            ref = mem_refs[b // 2]
            span = slice(b * rows, (b + 1) * rows)
            k_all[h, span, :HEAD_DIM] = ref[b % 2, 0, :, head_cols(h)]
            k_all[h, span, HEAD_DIM:] = jnp.where(lane == b, NEG, 0.0).astype(BF16)
            v_all[h, span, :HEAD_DIM] = ref[b % 2, 1, :, head_cols(h)]
            v_all[h, span, HEAD_DIM:] = jnp.ones((rows, HEAD_DIM), BF16)
    spread = (
        lax.broadcasted_iota(jnp.int32, (tok, groups), 0) // (tok // groups)
        == lax.broadcasted_iota(jnp.int32, (tok, groups), 1)
    )
    spread = jnp.where(spread, 1.0, 0.0).astype(BF16)
    pad = jnp.zeros((HEAD_DIM - extra, groups), BF16)

    units = [(first, h) for first in range(0, peers, TILE) for h in range(PAIR)]
    shunned, scores, weights, parts = {}, {}, {}, [0.0] * PAIR
    for step in range(len(units) + 2):
        if step < len(units):
            first, h = units[step]
            if first not in shunned:
                shun = [
                    jnp.concatenate([got[first + t][2 * tok :, :groups], pad], axis=0)
                    for t in range(TILE)
                ]
                shunned[first] = jnp.concatenate(
                    [dot(spread, x, NT).astype(BF16) for x in shun], axis=0
                )
            q = tile_rows(got, first, 0, tok, head_cols(h))
            scores[step] = dot(jnp.concatenate([q, shunned[first]], axis=1), k_all[h], NT)
        if 1 <= step <= len(units):
            u = step - 1
            first, h = units[u]
            gate = gate_of(gate_ref, h)
            s = scores.pop(u)
            peak = jnp.max(s, axis=1, keepdims=True)
            e = jnp.exp2((s - peak) * (scale * LOG2E)).astype(BF16)
            o = dot(e, v_all[h])
            inv = 1.0 / o[:, HEAD_DIM:]
            o = o[:, :HEAD_DIM] * inv
            g32 = tile_rows(got, first, tok, tok, head_cols(h)).astype(F32)
            dout = (gate * g32).astype(BF16)
            delta = row_sums(dout.astype(F32) * o)
            mixed = (gate * o).astype(BF16)
            for t in range(TILE):
                back[first + t][:tok, head_cols(h)] = mixed[t * tok : (t + 1) * tok]
            parts[h] = parts[h] + jnp.sum(g32 * o, axis=0, keepdims=True)
            weights[u] = (e, dout, delta, inv)
        if 2 <= step:
            u = step - 2
            first, h = units[u]
            dq = backward(scale, *weights.pop(u), k_all, v_all, h)
            for t in range(TILE):
                back[first + t][tok : 2 * tok, head_cols(h)] = dq[t * tok : (t + 1) * tok]

    head = lax.broadcasted_iota(jnp.int32, (heads, HEAD_DIM), 0)
    total = before_ref[...]
    for h in range(PAIR):
        total = total + jnp.where(head == plane_index() * PAIR + h, parts[h], 0.0)
    total = jnp.sum(total, axis=1, keepdims=True)
    high = total.astype(BF16).astype(F32)
    middle = (total - high).astype(BF16).astype(F32)
    low = total - high - middle
    lane = lax.broadcasted_iota(jnp.int32, (heads, CHUNK), 1)
    terms = jnp.where(lane == 0, high, jnp.where(lane == 1, middle, jnp.where(lane == 2, low, 0.0)))
    for reply in back:
        reply[2 * tok :, :] = terms.astype(BF16)


def merge_kernel(lo_ref, ldq_ref, *refs):
    *back_refs, out_ref, dq_ref = refs
    back_refs = arrivals_of(back_refs)
    tok = lo_ref.shape[0]
    chunk = plane_index()
    for k, back_ref in enumerate(back_refs):
        cols = chunk_columns(chunk ^ k)
        for t, (ref, local_ref) in enumerate(((out_ref, lo_ref), (dq_ref, ldq_ref))):
            arrived = back_ref[t * tok : (t + 1) * tok].astype(F32)
            ref[:, cols] = (arrived + local_ref[:, cols].astype(F32)).astype(BF16)


def send_xor(array, axes, k):
    return lax.ppermute(array, axes, [(i, i ^ k) for i in range(lax.axis_size(axes))])


def spread_along(array, axis, ready):
    held = {0: array}
    step = lax.axis_size(axis) // 2
    while step:
        for k in sorted(held):
            source = held[k]
            if k and step == 1:
                source, held[1], ready = lax.optimization_barrier((source, held[1], ready))
            held[k + step] = send_xor(source, axis, step)
        step //= 2
    return held, ready


def across(pairs):
    order = reversed(range(len(pairs)))
    return [send_xor(pairs[i], PLANE, 2 * i + 2) for i in order][::-1]


def forward(pairs):
    return [x for pair in pairs for x in (pair, send_xor(pair, PLANE, 1))]


def sum_over(array, axis):
    arrived = [send_xor(array, axis, k) for k in range(1, lax.axis_size(axis))]
    return functools.reduce(jnp.add, arrived, array)


def body(query, key, value, mem_key, mem_value, block_ids, gate_logit, d_out):
    tok, width = query.shape
    heads = gate_logit.shape[0]
    scale = HEAD_DIM ** (-0.5)
    rows = mem_key.shape[0]
    groups = block_ids.shape[0]
    blocks = lax.axis_size(MEM)
    peers = width // CHUNK
    devices = lax.axis_size(ALL)

    params = pltpu.CompilerParams(vmem_limit_bytes=(6 + 5 * blocks // 4) * MIB)
    alone = pltpu.CompilerParams(vmem_limit_bytes=60 * MIB)
    hbm_spec = pl.BlockSpec(memory_space=pltpu.HBM)
    vmem_spec = pl.BlockSpec(memory_space=pltpu.VMEM)
    packet = jax.ShapeDtypeStruct((2 * tok + max(16, blocks), CHUNK), BF16)
    pairs = peers // 2 - 1
    chunk_shape = jax.ShapeDtypeStruct((2, rows, CHUNK), BF16)
    mine, theirs, *send = pl.pallas_call(
        functools.partial(prologue_kernel, blocks),
        out_shape=(chunk_shape,) * 2 + (packet,) * peers,
        in_specs=[hbm_spec] * 4 + [vmem_spec],
        out_specs=(vmem_spec,) * (2 + peers),
        scratch_shapes=[pltpu.SemaphoreType.DMA((2, 2)), pltpu.SemaphoreType.DMA((peers, 2))],
        compiler_params=alone,
        name="chunks",
    )(mem_key, mem_value, query, d_out, jnp.transpose(block_ids))
    both = pl.pallas_call(
        join_kernel,
        out_shape=jax.ShapeDtypeStruct((2,) + chunk_shape.shape, BF16),
        in_specs=[vmem_spec] * 2,
        out_specs=vmem_spec,
        compiler_params=params,
        name="join_cores",
    )(mine, send_xor(theirs, "core", 1))

    gate = jax.nn.sigmoid(gate_logit)
    gate_cols = jnp.repeat(gate, HEAD_DIM)[None, :]
    steps = 4
    step_heads = heads // steps
    col_spec = pl.BlockSpec((tok, step_heads * HEAD_DIM), lambda j: (0, j))
    prob_spec = pl.BlockSpec((step_heads, tok, tok), lambda j: (j, 0, 0))
    local_out, local_prob, local_part = pl.pallas_call(
        functools.partial(local_forward_kernel, scale),
        grid=(steps,),
        out_shape=(
            jax.ShapeDtypeStruct((tok, width), F32),
            jax.ShapeDtypeStruct((heads, tok, tok), BF16),
            jax.ShapeDtypeStruct((steps, step_heads, HEAD_DIM), F32),
        ),
        in_specs=[col_spec] * 4,
        out_specs=(
            col_spec,
            prob_spec,
            pl.BlockSpec((1, step_heads, HEAD_DIM), lambda j: (j, 0, 0)),
        ),
        compiler_params=params,
        cost_estimate=pl.CostEstimate(
            flops=4 * heads * tok * tok * HEAD_DIM, bytes_accessed=12 * tok * width,
            transcendentals=heads * tok * tok,
        ),
        name="local_forward",
    )(query, key, value, d_out)

    got = list(send)
    for k in (6, 7, 5, 4, 2, 3, 1):
        got[k] = send_xor(send[k], PLANE, k)
    spread, (got[5:], local_part) = spread_along(both, "z", (got[5:], local_part))
    memory = [spread[k] for k in range(blocks // 2)]

    whole = jax.ShapeDtypeStruct((tok, width), BF16)
    local_mix, local_dq = pl.pallas_call(
        functools.partial(local_backward_kernel, scale),
        grid=(steps,),
        out_shape=(whole, whole),
        in_specs=[col_spec] * 3
        + [pl.BlockSpec((1, step_heads * HEAD_DIM), lambda j: (0, j)), col_spec, prob_spec],
        out_specs=(col_spec, col_spec),
        compiler_params=params,
        cost_estimate=pl.CostEstimate(
            flops=4 * heads * tok * tok * HEAD_DIM, bytes_accessed=16 * tok * width,
            transcendentals=0,
        ),
        name="local_backward",
    )(key, value, d_out, gate_cols, local_out, local_prob)
    memory, local_mix, local_dq = lax.optimization_barrier((memory, local_mix, local_dq))

    keys_shape = (PAIR, blocks * rows, CHUNK)

    reply = jax.ShapeDtypeStruct((2 * tok + heads, CHUNK), BF16)
    pair_reply = jax.ShapeDtypeStruct((2,) + reply.shape, BF16)
    replies = pl.pallas_call(
        functools.partial(attend_kernel, scale, groups, peers),
        out_shape=(reply,) * 2 + (pair_reply,) * pairs,
        in_specs=[vmem_spec] * (2 + peers + blocks // 2),
        out_specs=(vmem_spec,) * (2 + pairs),
        scratch_shapes=[pltpu.VMEM(keys_shape, BF16), pltpu.VMEM(keys_shape, BF16)],
        compiler_params=params,
        cost_estimate=pl.CostEstimate(
            flops=8 * peers * tok * blocks * rows * CHUNK, bytes_accessed=10 * tok * width,
            transcendentals=heads * tok * blocks * rows,
        ),
        name="memory_attention",
    )(gate_cols, -local_part.reshape(heads, HEAD_DIM), *got, *memory)
    back = [replies[0], send_xor(replies[1], PLANE, 1)] + forward(across(replies[2:]))

    rows_of = [x[2 * tok :, :HEAD_DIM] for x in back[:2]]
    rows_of += [x[i % 2, 2 * tok :, :HEAD_DIM] for i, x in enumerate(back[2:])]
    sums = functools.reduce(jnp.add, [x.astype(F32) for x in rows_of])
    sums = jnp.sum(sum_over(sum_over(sums, "z"), "sa")[:, :3], axis=1)
    gate_grad = sums * gate * (1.0 - gate) / math.sqrt(tok * devices)

    out, d_query = pl.pallas_call(
        merge_kernel,
        out_shape=(whole, whole),
        in_specs=[vmem_spec] * (2 + peers),
        out_specs=(vmem_spec, vmem_spec),
        compiler_params=params,
        name="merge",
    )(local_mix, local_dq, *back)
    return (out, d_query, gate_grad)


def solution(mesh):
    seq, mem = mesh.devices.shape
    sb = min(seq, 4)
    fine = Mesh(mesh.devices.reshape(seq // sb, sb, mem // 2, 2), ALL)
    tokens = P(ALL, None)
    blocks = P(MEM, None)
    return jax.shard_map(
        body,
        mesh=fine,
        in_specs=(tokens, tokens, tokens, blocks, blocks, tokens, P(), tokens),
        out_specs=(tokens, tokens, P()),
        check_vma=False,
    )
```

```python
import functools
import math

import jax
import jax.numpy as jnp
from jax import lax
from jax.experimental import pallas as pl
from jax.experimental.pallas import tpu as pltpu
from jax.sharding import Mesh, PartitionSpec as P

HEAD_DIM = 128
PAIR = 2
CHUNK = PAIR * HEAD_DIM
TILE = 2
NEG = -1e30
LOG2E = math.log2(math.e)
MIB = 1024 * 1024
F32 = jnp.float32
BF16 = jnp.bfloat16
NT = (((1,), (1,)), ((), ()))
NN = (((1,), (0,)), ((), ()))
PLANE = ("sb", "core")
MEM = ("z", "core")
ALL = ("sa", "sb", "z", "core")


def dot(a, b, dims=NN):
    return lax.dot_general(a, b, dims, preferred_element_type=F32)


def head_cols(h):
    return slice(h * HEAD_DIM, (h + 1) * HEAD_DIM)


def chunk_columns(chunk):
    return pl.ds(pl.multiple_of(chunk * CHUNK, CHUNK), CHUNK)


def plane_index():
    return lax.axis_index("sb") * 2 + lax.axis_index("core")


def row_sums(x):
    high = x.astype(BF16)
    low = (x - high.astype(F32)).astype(BF16)
    return dot(jnp.concatenate([high, low], axis=1), jnp.ones((2 * HEAD_DIM, HEAD_DIM), BF16))


def packets_of(refs):
    own, core, *pairs = refs
    return [own, core] + [pair.at[lane] for pair in pairs for lane in range(2)]


def arrivals_of(refs):
    own, core, *pairs = refs
    return [own, core] + [pair.at[i % 2] for i, pair in enumerate(pairs)]


def prologue_kernel(
    blocks, mk_hbm, mv_hbm, q_hbm, g_hbm, ids_ref, mine_ref, theirs_ref, *refs
):
    *out_refs, mem_sems, in_sems = refs
    tok = q_hbm.shape[0]
    fetched, groups = ids_ref.shape
    chunk = plane_index()
    copies = [
        pltpu.make_async_copy(
            ref.at[:, chunk_columns(chunk ^ i)], out_ref.at[t], mem_sems.at[i, t]
        )
        for i, out_ref in enumerate((mine_ref, theirs_ref))
        for t, ref in enumerate((mk_hbm, mv_hbm))
    ]
    for k, packet in enumerate(out_refs):
        for t, ref in enumerate((q_hbm, g_hbm)):
            span = slice(t * tok, (t + 1) * tok)
            copies.append(
                pltpu.make_async_copy(
                    ref.at[:, chunk_columns(chunk ^ k)], packet.at[span], in_sems.at[k, t]
                )
            )
    for copy in copies:
        copy.start()
    row = lax.broadcasted_iota(jnp.int32, (out_refs[0].shape[0] - 2 * tok, groups), 0)
    owner = lax.axis_index("z") * 2 + lax.axis_index("core")
    for core in range(2):
        hot = row >= blocks
        for t in range(fetched):
            hot = hot | (row == (ids_ref[t : t + 1, :] ^ owner ^ core))
        shun = jnp.where(hot, 0.0, 1.0).astype(BF16)
        for packet in out_refs[core::2]:
            packet[2 * tok :, :groups] = shun
    for copy in copies:
        copy.wait()


def join_kernel(mine_ref, other_ref, out_ref):
    out_ref[0] = mine_ref[...]
    out_ref[1] = other_ref[...]


def local_forward_kernel(scale, q_ref, k_ref, v_ref, g_ref, out_ref, prob_ref, part_ref):
    tok = q_ref.shape[0]
    heads = part_ref.shape[1]
    row = lax.broadcasted_iota(jnp.int32, (tok, tok), 0)
    col = lax.broadcasted_iota(jnp.int32, (tok, tok), 1)
    causal = row >= col
    s = [dot(q_ref[:, head_cols(h)], k_ref[:, head_cols(h)], NT) for h in range(heads)]
    s = [jnp.where(causal, x, NEG) for x in s]
    e = [jnp.exp2((x - jnp.max(x, axis=1, keepdims=True)) * (scale * LOG2E)) for x in s]
    p = [x * (1.0 / row_sums(x)) for x in e]
    p = [x.astype(BF16) for x in p]
    for h in range(heads):
        cols = head_cols(h)
        o = dot(p[h], v_ref[:, cols])
        prob_ref[h] = p[h]
        out_ref[:, cols] = o
        part_ref[0, h : h + 1, :] = jnp.sum(g_ref[:, cols].astype(F32) * o, axis=0, keepdims=True)


def local_backward_kernel(scale, k_ref, v_ref, g_ref, gate_ref, out_ref, prob_ref, lo_ref, dq_ref):
    heads = prob_ref.shape[0]
    for h in range(heads):
        shut = 1.0 - gate_ref[:, head_cols(h)]
        lo_ref[:, head_cols(h)] = (shut * out_ref[:, head_cols(h)]).astype(BF16)
    dout = [
        ((1.0 - gate_ref[:, head_cols(h)]) * g_ref[:, head_cols(h)].astype(F32)).astype(BF16)
        for h in range(heads)
    ]
    delta = [row_sums(dout[h].astype(F32) * out_ref[:, head_cols(h)]) for h in range(heads)]
    dp = [dot(dout[h], v_ref[:, head_cols(h)], NT) for h in range(heads)]
    for h in range(heads):
        ds = (prob_ref[h].astype(F32) * (dp[h] - delta[h])).astype(BF16)
        dq_ref[:, head_cols(h)] = (dot(ds, k_ref[:, head_cols(h)]) * scale).astype(BF16)


def tile_rows(packets, first, start, count, cols):
    return jnp.concatenate(
        [packets[first + t][start : start + count, cols] for t in range(TILE)], axis=0
    )


def gate_of(gate_ref, h):
    return gate_ref[:, chunk_columns(plane_index())][:, head_cols(h)]


def backward(scale, e, dout, delta, inv, k_ref, v_ref, h):
    keys = k_ref.shape[1]
    dp = dot(dout, v_ref[h, :, :HEAD_DIM], NT)
    delta = jnp.concatenate([delta] * (keys // HEAD_DIM), axis=1)
    ds = (e.astype(F32) * (dp - delta)).astype(BF16)
    return (dot(ds, k_ref[h, :, :HEAD_DIM]) * (inv * scale)).astype(BF16)


def attend_kernel(scale, groups, peers, gate_ref, before_ref, *refs):
    *refs, part_ref, k_all, v_all = refs
    got, refs = refs[:peers], refs[peers:]
    pairs = peers // 2 - 1
    mem_refs, back = refs[: -pairs - 2], packets_of(refs[-pairs - 2 :])
    rows = mem_refs[0].shape[2]
    heads = before_ref.shape[0]
    tok = back[0].shape[0] // 2
    extra = got[0].shape[0] - 2 * tok
    lane = lax.broadcasted_iota(jnp.int32, (rows, HEAD_DIM), 1)
    for h in range(PAIR):
        for b in range(2 * len(mem_refs)):
            ref = mem_refs[b // 2]
            span = slice(b * rows, (b + 1) * rows)
            k_all[h, span, :HEAD_DIM] = ref[b % 2, 0, :, head_cols(h)]
            k_all[h, span, HEAD_DIM:] = jnp.where(lane == b, NEG, 0.0).astype(BF16)
            v_all[h, span, :HEAD_DIM] = ref[b % 2, 1, :, head_cols(h)]
            v_all[h, span, HEAD_DIM:] = jnp.ones((rows, HEAD_DIM), BF16)
    spread = (
        lax.broadcasted_iota(jnp.int32, (tok, groups), 0) // (tok // groups)
        == lax.broadcasted_iota(jnp.int32, (tok, groups), 1)
    )
    spread = jnp.where(spread, 1.0, 0.0).astype(BF16)
    pad = jnp.zeros((HEAD_DIM - extra, groups), BF16)

    units = [(first, h) for first in range(0, peers, TILE) for h in range(PAIR)]
    shunned, scores, weights, parts = {}, {}, {}, [0.0] * PAIR
    for step in range(len(units) + 2):
        if step < len(units):
            first, h = units[step]
            if first not in shunned:
                shun = [
                    jnp.concatenate([got[first + t][2 * tok :, :groups], pad], axis=0)
                    for t in range(TILE)
                ]
                shunned[first] = jnp.concatenate(
                    [dot(spread, x, NT).astype(BF16) for x in shun], axis=0
                )
            q = tile_rows(got, first, 0, tok, head_cols(h))
            scores[step] = dot(jnp.concatenate([q, shunned[first]], axis=1), k_all[h], NT)
        if 1 <= step <= len(units):
            u = step - 1
            first, h = units[u]
            gate = gate_of(gate_ref, h)
            s = scores.pop(u)
            peak = jnp.max(s, axis=1, keepdims=True)
            e = jnp.exp2((s - peak) * (scale * LOG2E)).astype(BF16)
            o = dot(e, v_all[h])
            inv = 1.0 / o[:, HEAD_DIM:]
            o = o[:, :HEAD_DIM] * inv
            g32 = tile_rows(got, first, tok, tok, head_cols(h)).astype(F32)
            dout = (gate * g32).astype(BF16)
            delta = row_sums(dout.astype(F32) * o)
            mixed = (gate * o).astype(BF16)
            for t in range(TILE):
                back[first + t][:tok, head_cols(h)] = mixed[t * tok : (t + 1) * tok]
            parts[h] = parts[h] + jnp.sum(g32 * o, axis=0, keepdims=True)
            weights[u] = (e, dout, delta, inv)
        if 2 <= step:
            u = step - 2
            first, h = units[u]
            dq = backward(scale, *weights.pop(u), k_all, v_all, h)
            for t in range(TILE):
                back[first + t][tok : 2 * tok, head_cols(h)] = dq[t * tok : (t + 1) * tok]

    head = lax.broadcasted_iota(jnp.int32, (heads, HEAD_DIM), 0)
    total = before_ref[...]
    for h in range(PAIR):
        total = total + jnp.where(head == plane_index() * PAIR + h, parts[h], 0.0)
    part_ref[...] = total


def merge_kernel(lo_ref, ldq_ref, *refs):
    *back_refs, out_ref, dq_ref = refs
    back_refs = arrivals_of(back_refs)
    tok = lo_ref.shape[0]
    chunk = plane_index()
    for k, back_ref in enumerate(back_refs):
        cols = chunk_columns(chunk ^ k)
        for t, (ref, local_ref) in enumerate(((out_ref, lo_ref), (dq_ref, ldq_ref))):
            arrived = back_ref[t * tok : (t + 1) * tok].astype(F32)
            ref[:, cols] = (arrived + local_ref[:, cols].astype(F32)).astype(BF16)


def send_xor(array, axes, k):
    return lax.ppermute(array, axes, [(i, i ^ k) for i in range(lax.axis_size(axes))])


def spread_along(array, axis, ready):
    held = {0: array}
    step = lax.axis_size(axis) // 2
    while step:
        for k in sorted(held):
            source = held[k]
            if k and step == 1:
                source, held[1], ready = lax.optimization_barrier((source, held[1], ready))
            held[k + step] = send_xor(source, axis, step)
        step //= 2
    return held, ready


def across(pairs):
    order = reversed(range(len(pairs)))
    return [send_xor(pairs[i], PLANE, 2 * i + 2) for i in order][::-1]


def forward(pairs):
    return [x for pair in pairs for x in (pair, send_xor(pair, PLANE, 1))]


def sum_over(array, axis):
    arrived = [send_xor(array, axis, k) for k in range(1, lax.axis_size(axis))]
    return functools.reduce(jnp.add, arrived, array)


def body(query, key, value, mem_key, mem_value, block_ids, gate_logit, d_out):
    tok, width = query.shape
    heads = gate_logit.shape[0]
    scale = HEAD_DIM ** (-0.5)
    rows = mem_key.shape[0]
    groups = block_ids.shape[0]
    blocks = lax.axis_size(MEM)
    peers = width // CHUNK
    devices = lax.axis_size(ALL)

    params = pltpu.CompilerParams(vmem_limit_bytes=(6 + 5 * blocks // 4) * MIB)
    alone = pltpu.CompilerParams(vmem_limit_bytes=60 * MIB)
    hbm_spec = pl.BlockSpec(memory_space=pltpu.HBM)
    vmem_spec = pl.BlockSpec(memory_space=pltpu.VMEM)
    packet = jax.ShapeDtypeStruct((2 * tok + max(16, blocks), CHUNK), BF16)
    pairs = peers // 2 - 1
    chunk_shape = jax.ShapeDtypeStruct((2, rows, CHUNK), BF16)
    mine, theirs, *send = pl.pallas_call(
        functools.partial(prologue_kernel, blocks),
        out_shape=(chunk_shape,) * 2 + (packet,) * peers,
        in_specs=[hbm_spec] * 4 + [vmem_spec],
        out_specs=(vmem_spec,) * (2 + peers),
        scratch_shapes=[pltpu.SemaphoreType.DMA((2, 2)), pltpu.SemaphoreType.DMA((peers, 2))],
        compiler_params=alone,
        name="chunks",
    )(mem_key, mem_value, query, d_out, jnp.transpose(block_ids))
    both = pl.pallas_call(
        join_kernel,
        out_shape=jax.ShapeDtypeStruct((2,) + chunk_shape.shape, BF16),
        in_specs=[vmem_spec] * 2,
        out_specs=vmem_spec,
        compiler_params=params,
        name="join_cores",
    )(mine, send_xor(theirs, "core", 1))

    gate = jax.nn.sigmoid(gate_logit)
    gate_cols = jnp.repeat(gate, HEAD_DIM)[None, :]
    steps = 4
    step_heads = heads // steps
    col_spec = pl.BlockSpec((tok, step_heads * HEAD_DIM), lambda j: (0, j))
    prob_spec = pl.BlockSpec((step_heads, tok, tok), lambda j: (j, 0, 0))
    local_out, local_prob, local_part = pl.pallas_call(
        functools.partial(local_forward_kernel, scale),
        grid=(steps,),
        out_shape=(
            jax.ShapeDtypeStruct((tok, width), F32),
            jax.ShapeDtypeStruct((heads, tok, tok), BF16),
            jax.ShapeDtypeStruct((steps, step_heads, HEAD_DIM), F32),
        ),
        in_specs=[col_spec] * 4,
        out_specs=(
            col_spec,
            prob_spec,
            pl.BlockSpec((1, step_heads, HEAD_DIM), lambda j: (j, 0, 0)),
        ),
        compiler_params=params,
        cost_estimate=pl.CostEstimate(
            flops=4 * heads * tok * tok * HEAD_DIM, bytes_accessed=12 * tok * width,
            transcendentals=heads * tok * tok,
        ),
        name="local_forward",
    )(query, key, value, d_out)

    got = list(send)
    for k in (6, 7, 5, 4, 2, 3, 1):
        got[k] = send_xor(send[k], PLANE, k)
    spread, (got[5:], local_part) = spread_along(both, "z", (got[5:], local_part))
    memory = [spread[k] for k in range(blocks // 2)]

    whole = jax.ShapeDtypeStruct((tok, width), BF16)
    local_mix, local_dq = pl.pallas_call(
        functools.partial(local_backward_kernel, scale),
        grid=(steps,),
        out_shape=(whole, whole),
        in_specs=[col_spec] * 3
        + [pl.BlockSpec((1, step_heads * HEAD_DIM), lambda j: (0, j)), col_spec, prob_spec],
        out_specs=(col_spec, col_spec),
        compiler_params=params,
        cost_estimate=pl.CostEstimate(
            flops=4 * heads * tok * tok * HEAD_DIM, bytes_accessed=16 * tok * width,
            transcendentals=0,
        ),
        name="local_backward",
    )(key, value, d_out, gate_cols, local_out, local_prob)
    memory, local_mix, local_dq = lax.optimization_barrier((memory, local_mix, local_dq))

    keys_shape = (PAIR, blocks * rows, CHUNK)

    reply = jax.ShapeDtypeStruct((2 * tok, CHUNK), BF16)
    pair_reply = jax.ShapeDtypeStruct((2,) + reply.shape, BF16)
    *replies, part = pl.pallas_call(
        functools.partial(attend_kernel, scale, groups, peers),
        out_shape=(reply,) * 2
        + (pair_reply,) * pairs
        + (jax.ShapeDtypeStruct((heads, HEAD_DIM), F32),),
        in_specs=[vmem_spec] * (2 + peers + blocks // 2),
        out_specs=(vmem_spec,) * (3 + pairs),
        scratch_shapes=[pltpu.VMEM(keys_shape, BF16), pltpu.VMEM(keys_shape, BF16)],
        compiler_params=params,
        cost_estimate=pl.CostEstimate(
            flops=8 * peers * tok * blocks * rows * CHUNK, bytes_accessed=10 * tok * width,
            transcendentals=heads * tok * blocks * rows,
        ),
        name="memory_attention",
    )(gate_cols, -local_part.reshape(heads, HEAD_DIM), *got, *memory)
    arrived = across(replies[2:])
    core_back = send_xor(replies[1], PLANE, 1)
    core_back, arrived[0] = lax.optimization_barrier((core_back, arrived[0]))
    back = [replies[0], core_back] + forward(arrived)

    sums = sum_over(sum_over(part, "z"), "sa")
    for step in (1, 2, 4):
        sums = sums + send_xor(sums, PLANE, step)
    sums = jnp.sum(sums, axis=1)
    gate_grad = sums * gate * (1.0 - gate) / math.sqrt(tok * devices)

    out, d_query = pl.pallas_call(
        merge_kernel,
        out_shape=(whole, whole),
        in_specs=[vmem_spec] * (2 + peers),
        out_specs=(vmem_spec, vmem_spec),
        compiler_params=params,
        name="merge",
    )(local_mix, local_dq, *back)
    return (out, d_query, gate_grad)


def solution(mesh):
    seq, mem = mesh.devices.shape
    sb = min(seq, 4)
    fine = Mesh(mesh.devices.reshape(seq // sb, sb, mem // 2, 2), ALL)
    tokens = P(ALL, None)
    blocks = P(MEM, None)
    return jax.shard_map(
        body,
        mesh=fine,
        in_specs=(tokens, tokens, tokens, blocks, blocks, tokens, P(), tokens),
        out_specs=(tokens, tokens, P()),
        check_vma=False,
    )
```

```python
import functools
import math

import jax
import jax.numpy as jnp
from jax import lax
from jax.experimental import pallas as pl
from jax.experimental.pallas import tpu as pltpu
from jax.sharding import Mesh, PartitionSpec as P

HEAD_DIM = 128
PAIR = 2
CHUNK = PAIR * HEAD_DIM
TILE = 2
NEG = -1e30
LOG2E = math.log2(math.e)
MIB = 1024 * 1024
F32 = jnp.float32
BF16 = jnp.bfloat16
NT = (((1,), (1,)), ((), ()))
NN = (((1,), (0,)), ((), ()))
PLANE = ("sb", "core")
MEM = ("z", "core")
ALL = ("sa", "sb", "z", "core")


def dot(a, b, dims=NN):
    return lax.dot_general(a, b, dims, preferred_element_type=F32)


def head_cols(h):
    return slice(h * HEAD_DIM, (h + 1) * HEAD_DIM)


def chunk_columns(chunk):
    return pl.ds(pl.multiple_of(chunk * CHUNK, CHUNK), CHUNK)


def plane_index():
    return lax.axis_index("sb") * 2 + lax.axis_index("core")


def row_sums(x):
    high = x.astype(BF16)
    low = (x - high.astype(F32)).astype(BF16)
    return dot(jnp.concatenate([high, low], axis=1), jnp.ones((2 * HEAD_DIM, HEAD_DIM), BF16))


def packets_of(refs):
    own, core, *pairs = refs
    return [own, core] + [pair.at[lane] for pair in pairs for lane in range(2)]


def arrivals_of(refs):
    own, core, *pairs = refs
    return [own, core] + [pair.at[i % 2] for i, pair in enumerate(pairs)]


def prologue_kernel(
    blocks, mk_hbm, mv_hbm, q_hbm, g_hbm, ids_ref, mine_ref, theirs_ref, *refs
):
    *out_refs, mem_sems, in_sems = refs
    tok = q_hbm.shape[0]
    fetched, groups = ids_ref.shape
    chunk = plane_index()
    copies = [
        pltpu.make_async_copy(
            ref.at[:, chunk_columns(chunk ^ i)], out_ref.at[t], mem_sems.at[i, t]
        )
        for i, out_ref in enumerate((mine_ref, theirs_ref))
        for t, ref in enumerate((mk_hbm, mv_hbm))
    ]
    for k, packet in enumerate(out_refs):
        for t, ref in enumerate((q_hbm, g_hbm)):
            span = slice(t * tok, (t + 1) * tok)
            copies.append(
                pltpu.make_async_copy(
                    ref.at[:, chunk_columns(chunk ^ k)], packet.at[span], in_sems.at[k, t]
                )
            )
    for copy in copies:
        copy.start()
    row = lax.broadcasted_iota(jnp.int32, (out_refs[0].shape[0] - 2 * tok, groups), 0)
    owner = lax.axis_index("z") * 2 + lax.axis_index("core")
    for core in range(2):
        hot = row >= blocks
        for t in range(fetched):
            hot = hot | (row == (ids_ref[t : t + 1, :] ^ owner ^ core))
        shun = jnp.where(hot, 0.0, 1.0).astype(BF16)
        for packet in out_refs[core::2]:
            packet[2 * tok :, :groups] = shun
    for copy in copies:
        copy.wait()


def join_kernel(mine_ref, other_ref, out_ref):
    out_ref[0] = mine_ref[...]
    out_ref[1] = other_ref[...]


def local_forward_kernel(scale, q_ref, k_ref, v_ref, g_ref, out_ref, prob_ref, part_ref):
    tok = q_ref.shape[0]
    heads = part_ref.shape[1]
    row = lax.broadcasted_iota(jnp.int32, (tok, tok), 0)
    col = lax.broadcasted_iota(jnp.int32, (tok, tok), 1)
    causal = row >= col
    s = [dot(q_ref[:, head_cols(h)], k_ref[:, head_cols(h)], NT) for h in range(heads)]
    s = [jnp.where(causal, x, NEG) for x in s]
    e = [jnp.exp2((x - jnp.max(x, axis=1, keepdims=True)) * (scale * LOG2E)) for x in s]
    p = [x * (1.0 / row_sums(x)) for x in e]
    p = [x.astype(BF16) for x in p]
    for h in range(heads):
        cols = head_cols(h)
        o = dot(p[h], v_ref[:, cols])
        prob_ref[h] = p[h]
        out_ref[:, cols] = o
        part_ref[0, h : h + 1, :] = jnp.sum(g_ref[:, cols].astype(F32) * o, axis=0, keepdims=True)


def local_backward_kernel(scale, k_ref, v_ref, g_ref, gate_ref, out_ref, prob_ref, lo_ref, dq_ref):
    heads = prob_ref.shape[0]
    for h in range(heads):
        shut = 1.0 - gate_ref[:, head_cols(h)]
        lo_ref[:, head_cols(h)] = (shut * out_ref[:, head_cols(h)]).astype(BF16)
    dout = [
        ((1.0 - gate_ref[:, head_cols(h)]) * g_ref[:, head_cols(h)].astype(F32)).astype(BF16)
        for h in range(heads)
    ]
    delta = [row_sums(dout[h].astype(F32) * out_ref[:, head_cols(h)]) for h in range(heads)]
    dp = [dot(dout[h], v_ref[:, head_cols(h)], NT) for h in range(heads)]
    for h in range(heads):
        ds = (prob_ref[h].astype(F32) * (dp[h] - delta[h])).astype(BF16)
        dq_ref[:, head_cols(h)] = (dot(ds, k_ref[:, head_cols(h)]) * scale).astype(BF16)


def tile_rows(packets, first, start, count, cols):
    return jnp.concatenate(
        [packets[first + t][start : start + count, cols] for t in range(TILE)], axis=0
    )


def gate_of(gate_ref, h):
    return gate_ref[:, chunk_columns(plane_index())][:, head_cols(h)]


def backward(scale, e, dout, delta, inv, k_ref, v_ref, h):
    keys = k_ref.shape[1]
    dp = dot(dout, v_ref[h, :, :HEAD_DIM], NT)
    delta = jnp.concatenate([delta] * (keys // HEAD_DIM), axis=1)
    ds = (e.astype(F32) * (dp - delta)).astype(BF16)
    return (dot(ds, k_ref[h, :, :HEAD_DIM]) * (inv * scale)).astype(BF16)


def attend_kernel(scale, groups, peers, gate_ref, before_ref, *refs):
    *refs, part_ref, k_all, v_all = refs
    got, refs = refs[:peers], refs[peers:]
    pairs = peers // 2 - 1
    mem_refs, back = refs[: -pairs - 2], packets_of(refs[-pairs - 2 :])
    rows = mem_refs[0].shape[2]
    heads = before_ref.shape[0]
    tok = back[0].shape[0] // 2
    extra = got[0].shape[0] - 2 * tok
    lane = lax.broadcasted_iota(jnp.int32, (rows, HEAD_DIM), 1)
    for h in range(PAIR):
        for b in range(2 * len(mem_refs)):
            ref = mem_refs[b // 2]
            span = slice(b * rows, (b + 1) * rows)
            k_all[h, span, :HEAD_DIM] = ref[b % 2, 0, :, head_cols(h)]
            k_all[h, span, HEAD_DIM:] = jnp.where(lane == b, NEG, 0.0).astype(BF16)
            v_all[h, span, :HEAD_DIM] = ref[b % 2, 1, :, head_cols(h)]
            v_all[h, span, HEAD_DIM:] = jnp.ones((rows, HEAD_DIM), BF16)
    spread = (
        lax.broadcasted_iota(jnp.int32, (tok, groups), 0) // (tok // groups)
        == lax.broadcasted_iota(jnp.int32, (tok, groups), 1)
    )
    spread = jnp.where(spread, 1.0, 0.0).astype(BF16)
    pad = jnp.zeros((HEAD_DIM - extra, groups), BF16)

    units = [(first, h) for first in range(0, peers, TILE) for h in range(PAIR)]
    shunned, scores, weights, parts = {}, {}, {}, [0.0] * PAIR
    for step in range(len(units) + 2):
        if step < len(units):
            first, h = units[step]
            if first not in shunned:
                shun = [
                    jnp.concatenate([got[first + t][2 * tok :, :groups], pad], axis=0)
                    for t in range(TILE)
                ]
                shunned[first] = jnp.concatenate(
                    [dot(spread, x, NT).astype(BF16) for x in shun], axis=0
                )
            q = tile_rows(got, first, 0, tok, head_cols(h))
            scores[step] = dot(jnp.concatenate([q, shunned[first]], axis=1), k_all[h], NT)
        if 1 <= step <= len(units):
            u = step - 1
            first, h = units[u]
            gate = gate_of(gate_ref, h)
            s = scores.pop(u)
            peak = jnp.max(s, axis=1, keepdims=True)
            e = jnp.exp2((s - peak) * (scale * LOG2E)).astype(BF16)
            o = dot(e, v_all[h])
            inv = 1.0 / o[:, HEAD_DIM:]
            o = o[:, :HEAD_DIM] * inv
            g32 = tile_rows(got, first, tok, tok, head_cols(h)).astype(F32)
            dout = (gate * g32).astype(BF16)
            delta = row_sums(dout.astype(F32) * o)
            mixed = (gate * o).astype(BF16)
            for t in range(TILE):
                back[first + t][:tok, head_cols(h)] = mixed[t * tok : (t + 1) * tok]
            parts[h] = parts[h] + jnp.sum(g32 * o, axis=0, keepdims=True)
            weights[u] = (e, dout, delta, inv)
        if 2 <= step:
            u = step - 2
            first, h = units[u]
            dq = backward(scale, *weights.pop(u), k_all, v_all, h)
            for t in range(TILE):
                back[first + t][tok : 2 * tok, head_cols(h)] = dq[t * tok : (t + 1) * tok]

    head = lax.broadcasted_iota(jnp.int32, (heads, HEAD_DIM), 0)
    total = before_ref[...]
    for h in range(PAIR):
        total = total + jnp.where(head == plane_index() * PAIR + h, parts[h], 0.0)
    part_ref[...] = total


def merge_kernel(lo_ref, ldq_ref, *refs):
    *back_refs, out_ref, dq_ref = refs
    back_refs = arrivals_of(back_refs)
    tok = lo_ref.shape[0]
    chunk = plane_index()
    for k, back_ref in enumerate(back_refs):
        cols = chunk_columns(chunk ^ k)
        for t, (ref, local_ref) in enumerate(((out_ref, lo_ref), (dq_ref, ldq_ref))):
            arrived = back_ref[t * tok : (t + 1) * tok].astype(F32)
            ref[:, cols] = (arrived + local_ref[:, cols].astype(F32)).astype(BF16)


def send_xor(array, axes, k):
    return lax.ppermute(array, axes, [(i, i ^ k) for i in range(lax.axis_size(axes))])


def spread_along(array, axis, ready):
    held = {0: array}
    step = lax.axis_size(axis) // 2
    while step:
        for k in sorted(held):
            source = held[k]
            if k and step == 1:
                source, held[1], ready = lax.optimization_barrier((source, held[1], ready))
            held[k + step] = send_xor(source, axis, step)
        step //= 2
    return held, ready


def across(pairs):
    order = reversed(range(len(pairs)))
    return [send_xor(pairs[i], PLANE, 2 * i + 2) for i in order][::-1]


def forward(pairs):
    return [x for pair in pairs for x in (pair, send_xor(pair, PLANE, 1))]


def sum_over(array, axis):
    arrived = [send_xor(array, axis, k) for k in range(1, lax.axis_size(axis))]
    return functools.reduce(jnp.add, arrived, array)


def body(query, key, value, mem_key, mem_value, block_ids, gate_logit, d_out):
    tok, width = query.shape
    heads = gate_logit.shape[0]
    scale = HEAD_DIM ** (-0.5)
    rows = mem_key.shape[0]
    groups = block_ids.shape[0]
    blocks = lax.axis_size(MEM)
    peers = width // CHUNK
    devices = lax.axis_size(ALL)

    params = pltpu.CompilerParams(vmem_limit_bytes=(6 + 5 * blocks // 4) * MIB)
    alone = pltpu.CompilerParams(vmem_limit_bytes=60 * MIB)
    hbm_spec = pl.BlockSpec(memory_space=pltpu.HBM)
    vmem_spec = pl.BlockSpec(memory_space=pltpu.VMEM)
    packet = jax.ShapeDtypeStruct((2 * tok + max(16, blocks), CHUNK), BF16)
    pairs = peers // 2 - 1
    chunk_shape = jax.ShapeDtypeStruct((2, rows, CHUNK), BF16)
    mine, theirs, *send = pl.pallas_call(
        functools.partial(prologue_kernel, blocks),
        out_shape=(chunk_shape,) * 2 + (packet,) * peers,
        in_specs=[hbm_spec] * 4 + [vmem_spec],
        out_specs=(vmem_spec,) * (2 + peers),
        scratch_shapes=[pltpu.SemaphoreType.DMA((2, 2)), pltpu.SemaphoreType.DMA((peers, 2))],
        compiler_params=alone,
        name="chunks",
    )(mem_key, mem_value, query, d_out, jnp.transpose(block_ids))
    both = pl.pallas_call(
        join_kernel,
        out_shape=jax.ShapeDtypeStruct((2,) + chunk_shape.shape, BF16),
        in_specs=[vmem_spec] * 2,
        out_specs=vmem_spec,
        compiler_params=params,
        name="join_cores",
    )(mine, send_xor(theirs, "core", 1))

    gate = jax.nn.sigmoid(gate_logit)
    gate_cols = jnp.repeat(gate, HEAD_DIM)[None, :]
    steps = 4
    step_heads = heads // steps
    col_spec = pl.BlockSpec((tok, step_heads * HEAD_DIM), lambda j: (0, j))
    prob_spec = pl.BlockSpec((step_heads, tok, tok), lambda j: (j, 0, 0))
    local_out, local_prob, local_part = pl.pallas_call(
        functools.partial(local_forward_kernel, scale),
        grid=(steps,),
        out_shape=(
            jax.ShapeDtypeStruct((tok, width), F32),
            jax.ShapeDtypeStruct((heads, tok, tok), BF16),
            jax.ShapeDtypeStruct((steps, step_heads, HEAD_DIM), F32),
        ),
        in_specs=[col_spec] * 4,
        out_specs=(
            col_spec,
            prob_spec,
            pl.BlockSpec((1, step_heads, HEAD_DIM), lambda j: (j, 0, 0)),
        ),
        compiler_params=params,
        cost_estimate=pl.CostEstimate(
            flops=4 * heads * tok * tok * HEAD_DIM, bytes_accessed=12 * tok * width,
            transcendentals=heads * tok * tok,
        ),
        name="local_forward",
    )(query, key, value, d_out)

    got = list(send)
    for k in (6, 7, 5, 4, 2, 3, 1):
        got[k] = send_xor(send[k], PLANE, k)
    spread, (got[5:], local_part) = spread_along(both, "z", (got[5:], local_part))
    memory = [spread[k] for k in range(blocks // 2)]

    whole = jax.ShapeDtypeStruct((tok, width), BF16)
    local_mix, local_dq = pl.pallas_call(
        functools.partial(local_backward_kernel, scale),
        grid=(steps,),
        out_shape=(whole, whole),
        in_specs=[col_spec] * 3
        + [pl.BlockSpec((1, step_heads * HEAD_DIM), lambda j: (0, j)), col_spec, prob_spec],
        out_specs=(col_spec, col_spec),
        compiler_params=params,
        cost_estimate=pl.CostEstimate(
            flops=4 * heads * tok * tok * HEAD_DIM, bytes_accessed=16 * tok * width,
            transcendentals=0,
        ),
        name="local_backward",
    )(key, value, d_out, gate_cols, local_out, local_prob)
    memory, local_mix, local_dq = lax.optimization_barrier((memory, local_mix, local_dq))

    keys_shape = (PAIR, blocks * rows, CHUNK)

    reply = jax.ShapeDtypeStruct((2 * tok, CHUNK), BF16)
    pair_reply = jax.ShapeDtypeStruct((2,) + reply.shape, BF16)
    *replies, part = pl.pallas_call(
        functools.partial(attend_kernel, scale, groups, peers),
        out_shape=(reply,) * 2
        + (pair_reply,) * pairs
        + (jax.ShapeDtypeStruct((heads, HEAD_DIM), F32),),
        in_specs=[vmem_spec] * (2 + peers + blocks // 2),
        out_specs=(vmem_spec,) * (3 + pairs),
        scratch_shapes=[pltpu.VMEM(keys_shape, BF16), pltpu.VMEM(keys_shape, BF16)],
        compiler_params=params,
        cost_estimate=pl.CostEstimate(
            flops=8 * peers * tok * blocks * rows * CHUNK, bytes_accessed=10 * tok * width,
            transcendentals=heads * tok * blocks * rows,
        ),
        name="memory_attention",
    )(gate_cols, -local_part.reshape(heads, HEAD_DIM), *got, *memory)
    arrived = across(replies[2:])
    core_back = send_xor(replies[1], PLANE, 1)
    core_back, arrived[0] = lax.optimization_barrier((core_back, arrived[0]))
    back = [replies[0], core_back] + forward(arrived)

    sums = sum_over(sum_over(part, "z"), "sa")
    sums = sums + send_xor(sums, PLANE, 1)
    sums = functools.reduce(jnp.add, across([sums] * pairs), sums)
    sums = jnp.sum(sums, axis=1)
    gate_grad = sums * gate * (1.0 - gate) / math.sqrt(tok * devices)

    out, d_query = pl.pallas_call(
        merge_kernel,
        out_shape=(whole, whole),
        in_specs=[vmem_spec] * (2 + peers),
        out_specs=(vmem_spec, vmem_spec),
        compiler_params=params,
        name="merge",
    )(local_mix, local_dq, *back)
    return (out, d_query, gate_grad)


def solution(mesh):
    seq, mem = mesh.devices.shape
    sb = min(seq, 4)
    fine = Mesh(mesh.devices.reshape(seq // sb, sb, mem // 2, 2), ALL)
    tokens = P(ALL, None)
    blocks = P(MEM, None)
    return jax.shard_map(
        body,
        mesh=fine,
        in_specs=(tokens, tokens, tokens, blocks, blocks, tokens, P(), tokens),
        out_specs=(tokens, tokens, P()),
        check_vma=False,
    )
```

```python
import functools
import math

import jax
import jax.numpy as jnp
from jax import lax
from jax.experimental import pallas as pl
from jax.experimental.pallas import tpu as pltpu
from jax.sharding import Mesh, PartitionSpec as P

HEAD_DIM = 128
PAIR = 2
CHUNK = PAIR * HEAD_DIM
TILE = 4
NEG = -1e30
LOG2E = math.log2(math.e)
MIB = 1024 * 1024
F32 = jnp.float32
BF16 = jnp.bfloat16
NT = (((1,), (1,)), ((), ()))
NN = (((1,), (0,)), ((), ()))
PLANE = ("sb", "core")
MEM = ("z", "core")
ALL = ("sa", "sb", "z", "core")


def dot(a, b, dims=NN):
    return lax.dot_general(a, b, dims, preferred_element_type=F32)


def head_cols(h):
    return slice(h * HEAD_DIM, (h + 1) * HEAD_DIM)


def chunk_columns(chunk):
    return pl.ds(pl.multiple_of(chunk * CHUNK, CHUNK), CHUNK)


def plane_index():
    return lax.axis_index("sb") * 2 + lax.axis_index("core")


def row_sums(x):
    high = x.astype(BF16)
    low = (x - high.astype(F32)).astype(BF16)
    return dot(jnp.concatenate([high, low], axis=1), jnp.ones((2 * HEAD_DIM, HEAD_DIM), BF16))


def packets_of(refs):
    own, core, *pairs = refs
    return [own, core] + [pair.at[lane] for pair in pairs for lane in range(2)]


def arrivals_of(refs):
    own, core, *pairs = refs
    return [own, core] + [pair.at[i % 2] for i, pair in enumerate(pairs)]


def prologue_kernel(
    blocks, mk_hbm, mv_hbm, q_hbm, g_hbm, ids_ref, mine_ref, theirs_ref, *refs
):
    *out_refs, mem_sems, in_sems = refs
    tok = q_hbm.shape[0]
    fetched, groups = ids_ref.shape
    chunk = plane_index()
    copies = [
        pltpu.make_async_copy(
            ref.at[:, chunk_columns(chunk ^ i)], out_ref.at[t], mem_sems.at[i, t]
        )
        for i, out_ref in enumerate((mine_ref, theirs_ref))
        for t, ref in enumerate((mk_hbm, mv_hbm))
    ]
    for k, packet in enumerate(out_refs):
        for t, ref in enumerate((q_hbm, g_hbm)):
            span = slice(t * tok, (t + 1) * tok)
            copies.append(
                pltpu.make_async_copy(
                    ref.at[:, chunk_columns(chunk ^ k)], packet.at[span], in_sems.at[k, t]
                )
            )
    for copy in copies:
        copy.start()
    row = lax.broadcasted_iota(jnp.int32, (out_refs[0].shape[0] - 2 * tok, groups), 0)
    owner = lax.axis_index("z") * 2 + lax.axis_index("core")
    for core in range(2):
        hot = row >= blocks
        for t in range(fetched):
            hot = hot | (row == (ids_ref[t : t + 1, :] ^ owner ^ core))
        shun = jnp.where(hot, 0.0, 1.0).astype(BF16)
        for packet in out_refs[core::2]:
            packet[2 * tok :, :groups] = shun
    for copy in copies:
        copy.wait()


def join_kernel(mine_ref, other_ref, out_ref):
    out_ref[0] = mine_ref[...]
    out_ref[1] = other_ref[...]


def local_forward_kernel(scale, q_ref, k_ref, v_ref, g_ref, out_ref, prob_ref, part_ref):
    tok = q_ref.shape[0]
    heads = part_ref.shape[1]
    row = lax.broadcasted_iota(jnp.int32, (tok, tok), 0)
    col = lax.broadcasted_iota(jnp.int32, (tok, tok), 1)
    causal = row >= col
    s = [dot(q_ref[:, head_cols(h)], k_ref[:, head_cols(h)], NT) for h in range(heads)]
    s = [jnp.where(causal, x, NEG) for x in s]
    e = [jnp.exp2((x - jnp.max(x, axis=1, keepdims=True)) * (scale * LOG2E)) for x in s]
    p = [x * (1.0 / row_sums(x)) for x in e]
    p = [x.astype(BF16) for x in p]
    for h in range(heads):
        cols = head_cols(h)
        o = dot(p[h], v_ref[:, cols])
        prob_ref[h] = p[h]
        out_ref[:, cols] = o
        part_ref[0, h : h + 1, :] = jnp.sum(g_ref[:, cols].astype(F32) * o, axis=0, keepdims=True)


def local_backward_kernel(scale, k_ref, v_ref, g_ref, gate_ref, out_ref, prob_ref, lo_ref, dq_ref):
    heads = prob_ref.shape[0]
    for h in range(heads):
        shut = 1.0 - gate_ref[:, head_cols(h)]
        lo_ref[:, head_cols(h)] = (shut * out_ref[:, head_cols(h)]).astype(BF16)
    dout = [
        ((1.0 - gate_ref[:, head_cols(h)]) * g_ref[:, head_cols(h)].astype(F32)).astype(BF16)
        for h in range(heads)
    ]
    delta = [row_sums(dout[h].astype(F32) * out_ref[:, head_cols(h)]) for h in range(heads)]
    dp = [dot(dout[h], v_ref[:, head_cols(h)], NT) for h in range(heads)]
    for h in range(heads):
        ds = (prob_ref[h].astype(F32) * (dp[h] - delta[h])).astype(BF16)
        dq_ref[:, head_cols(h)] = (dot(ds, k_ref[:, head_cols(h)]) * scale).astype(BF16)


def tile_rows(packets, first, start, count, cols):
    return jnp.concatenate(
        [packets[first + t][start : start + count, cols] for t in range(TILE)], axis=0
    )


def gate_of(gate_ref, h):
    return gate_ref[:, chunk_columns(plane_index())][:, head_cols(h)]


def backward(scale, e, dout, delta, inv, k_ref, v_ref, h):
    keys = k_ref.shape[1]
    dp = dot(dout, v_ref[h, :, :HEAD_DIM], NT)
    delta = jnp.concatenate([delta] * (keys // HEAD_DIM), axis=1)
    ds = (e.astype(F32) * (dp - delta)).astype(BF16)
    return (dot(ds, k_ref[h, :, :HEAD_DIM]) * (inv * scale)).astype(BF16)


def attend_kernel(scale, groups, peers, gate_ref, before_ref, *refs):
    *refs, part_ref, k_all, v_all = refs
    got, refs = refs[:peers], refs[peers:]
    pairs = peers // 2 - 1
    mem_refs, back = refs[: -pairs - 2], packets_of(refs[-pairs - 2 :])
    rows = mem_refs[0].shape[2]
    heads = before_ref.shape[0]
    tok = back[0].shape[0] // 2
    extra = got[0].shape[0] - 2 * tok
    lane = lax.broadcasted_iota(jnp.int32, (rows, HEAD_DIM), 1)
    for h in range(PAIR):
        for b in range(2 * len(mem_refs)):
            ref = mem_refs[b // 2]
            span = slice(b * rows, (b + 1) * rows)
            k_all[h, span, :HEAD_DIM] = ref[b % 2, 0, :, head_cols(h)]
            k_all[h, span, HEAD_DIM:] = jnp.where(lane == b, NEG, 0.0).astype(BF16)
            v_all[h, span, :HEAD_DIM] = ref[b % 2, 1, :, head_cols(h)]
            v_all[h, span, HEAD_DIM:] = jnp.ones((rows, HEAD_DIM), BF16)
    spread = (
        lax.broadcasted_iota(jnp.int32, (tok, groups), 0) // (tok // groups)
        == lax.broadcasted_iota(jnp.int32, (tok, groups), 1)
    )
    spread = jnp.where(spread, 1.0, 0.0).astype(BF16)
    pad = jnp.zeros((HEAD_DIM - extra, groups), BF16)

    units = [(first, h) for first in range(0, peers, TILE) for h in range(PAIR)]
    shunned, scores, weights, parts = {}, {}, {}, [0.0] * PAIR
    for step in range(len(units) + 2):
        if step < len(units):
            first, h = units[step]
            if first not in shunned:
                shun = [
                    jnp.concatenate([got[first + t][2 * tok :, :groups], pad], axis=0)
                    for t in range(TILE)
                ]
                shunned[first] = jnp.concatenate(
                    [dot(spread, x, NT).astype(BF16) for x in shun], axis=0
                )
            q = tile_rows(got, first, 0, tok, head_cols(h))
            scores[step] = dot(jnp.concatenate([q, shunned[first]], axis=1), k_all[h], NT)
        if 1 <= step <= len(units):
            u = step - 1
            first, h = units[u]
            gate = gate_of(gate_ref, h)
            s = scores.pop(u)
            peak = jnp.max(s, axis=1, keepdims=True)
            e = jnp.exp2((s - peak) * (scale * LOG2E)).astype(BF16)
            o = dot(e, v_all[h])
            inv = 1.0 / o[:, HEAD_DIM:]
            o = o[:, :HEAD_DIM] * inv
            g32 = tile_rows(got, first, tok, tok, head_cols(h)).astype(F32)
            dout = (gate * g32).astype(BF16)
            delta = row_sums(dout.astype(F32) * o)
            mixed = (gate * o).astype(BF16)
            for t in range(TILE):
                back[first + t][:tok, head_cols(h)] = mixed[t * tok : (t + 1) * tok]
            parts[h] = parts[h] + jnp.sum(g32 * o, axis=0, keepdims=True)
            weights[u] = (e, dout, delta, inv)
        if 2 <= step:
            u = step - 2
            first, h = units[u]
            dq = backward(scale, *weights.pop(u), k_all, v_all, h)
            for t in range(TILE):
                back[first + t][tok : 2 * tok, head_cols(h)] = dq[t * tok : (t + 1) * tok]

    head = lax.broadcasted_iota(jnp.int32, (heads, HEAD_DIM), 0)
    total = before_ref[...]
    for h in range(PAIR):
        total = total + jnp.where(head == plane_index() * PAIR + h, parts[h], 0.0)
    part_ref[...] = total


def merge_kernel(lo_ref, ldq_ref, *refs):
    *back_refs, out_ref, dq_ref = refs
    back_refs = arrivals_of(back_refs)
    tok = lo_ref.shape[0]
    chunk = plane_index()
    for k, back_ref in enumerate(back_refs):
        cols = chunk_columns(chunk ^ k)
        for t, (ref, local_ref) in enumerate(((out_ref, lo_ref), (dq_ref, ldq_ref))):
            arrived = back_ref[t * tok : (t + 1) * tok].astype(F32)
            ref[:, cols] = (arrived + local_ref[:, cols].astype(F32)).astype(BF16)


def send_xor(array, axes, k):
    return lax.ppermute(array, axes, [(i, i ^ k) for i in range(lax.axis_size(axes))])


def spread_along(array, axis, ready):
    held = {0: array}
    step = lax.axis_size(axis) // 2
    while step:
        for k in sorted(held):
            source = held[k]
            if k and step == 1:
                source, held[1], ready = lax.optimization_barrier((source, held[1], ready))
            held[k + step] = send_xor(source, axis, step)
        step //= 2
    return held, ready


def across(pairs):
    order = reversed(range(len(pairs)))
    return [send_xor(pairs[i], PLANE, 2 * i + 2) for i in order][::-1]


def forward(pairs):
    return [x for pair in pairs for x in (pair, send_xor(pair, PLANE, 1))]


def sum_over(array, axis):
    arrived = [send_xor(array, axis, k) for k in range(1, lax.axis_size(axis))]
    return functools.reduce(jnp.add, arrived, array)


def body(query, key, value, mem_key, mem_value, block_ids, gate_logit, d_out):
    tok, width = query.shape
    heads = gate_logit.shape[0]
    scale = HEAD_DIM ** (-0.5)
    rows = mem_key.shape[0]
    groups = block_ids.shape[0]
    blocks = lax.axis_size(MEM)
    peers = width // CHUNK
    devices = lax.axis_size(ALL)

    params = pltpu.CompilerParams(vmem_limit_bytes=(6 + 5 * blocks // 4) * MIB)
    alone = pltpu.CompilerParams(vmem_limit_bytes=60 * MIB)
    hbm_spec = pl.BlockSpec(memory_space=pltpu.HBM)
    vmem_spec = pl.BlockSpec(memory_space=pltpu.VMEM)
    packet = jax.ShapeDtypeStruct((2 * tok + max(16, blocks), CHUNK), BF16)
    pairs = peers // 2 - 1
    chunk_shape = jax.ShapeDtypeStruct((2, rows, CHUNK), BF16)
    mine, theirs, *send = pl.pallas_call(
        functools.partial(prologue_kernel, blocks),
        out_shape=(chunk_shape,) * 2 + (packet,) * peers,
        in_specs=[hbm_spec] * 4 + [vmem_spec],
        out_specs=(vmem_spec,) * (2 + peers),
        scratch_shapes=[pltpu.SemaphoreType.DMA((2, 2)), pltpu.SemaphoreType.DMA((peers, 2))],
        compiler_params=alone,
        name="chunks",
    )(mem_key, mem_value, query, d_out, jnp.transpose(block_ids))
    both = pl.pallas_call(
        join_kernel,
        out_shape=jax.ShapeDtypeStruct((2,) + chunk_shape.shape, BF16),
        in_specs=[vmem_spec] * 2,
        out_specs=vmem_spec,
        compiler_params=params,
        name="join_cores",
    )(mine, send_xor(theirs, "core", 1))

    gate = jax.nn.sigmoid(gate_logit)
    gate_cols = jnp.repeat(gate, HEAD_DIM)[None, :]
    steps = 4
    step_heads = heads // steps
    col_spec = pl.BlockSpec((tok, step_heads * HEAD_DIM), lambda j: (0, j))
    prob_spec = pl.BlockSpec((step_heads, tok, tok), lambda j: (j, 0, 0))
    local_out, local_prob, local_part = pl.pallas_call(
        functools.partial(local_forward_kernel, scale),
        grid=(steps,),
        out_shape=(
            jax.ShapeDtypeStruct((tok, width), F32),
            jax.ShapeDtypeStruct((heads, tok, tok), BF16),
            jax.ShapeDtypeStruct((steps, step_heads, HEAD_DIM), F32),
        ),
        in_specs=[col_spec] * 4,
        out_specs=(
            col_spec,
            prob_spec,
            pl.BlockSpec((1, step_heads, HEAD_DIM), lambda j: (j, 0, 0)),
        ),
        compiler_params=params,
        cost_estimate=pl.CostEstimate(
            flops=4 * heads * tok * tok * HEAD_DIM, bytes_accessed=12 * tok * width,
            transcendentals=heads * tok * tok,
        ),
        name="local_forward",
    )(query, key, value, d_out)

    got = list(send)
    for k in (6, 7, 5, 4, 2, 3, 1):
        got[k] = send_xor(send[k], PLANE, k)
    spread, (got[5:], local_part) = spread_along(both, "z", (got[5:], local_part))
    memory = [spread[k] for k in range(blocks // 2)]

    whole = jax.ShapeDtypeStruct((tok, width), BF16)
    local_mix, local_dq = pl.pallas_call(
        functools.partial(local_backward_kernel, scale),
        grid=(steps,),
        out_shape=(whole, whole),
        in_specs=[col_spec] * 3
        + [pl.BlockSpec((1, step_heads * HEAD_DIM), lambda j: (0, j)), col_spec, prob_spec],
        out_specs=(col_spec, col_spec),
        compiler_params=params,
        cost_estimate=pl.CostEstimate(
            flops=4 * heads * tok * tok * HEAD_DIM, bytes_accessed=16 * tok * width,
            transcendentals=0,
        ),
        name="local_backward",
    )(key, value, d_out, gate_cols, local_out, local_prob)
    memory, local_mix, local_dq = lax.optimization_barrier((memory, local_mix, local_dq))

    keys_shape = (PAIR, blocks * rows, CHUNK)

    reply = jax.ShapeDtypeStruct((2 * tok, CHUNK), BF16)
    pair_reply = jax.ShapeDtypeStruct((2,) + reply.shape, BF16)
    *replies, part = pl.pallas_call(
        functools.partial(attend_kernel, scale, groups, peers),
        out_shape=(reply,) * 2
        + (pair_reply,) * pairs
        + (jax.ShapeDtypeStruct((heads, HEAD_DIM), F32),),
        in_specs=[vmem_spec] * (2 + peers + blocks // 2),
        out_specs=(vmem_spec,) * (3 + pairs),
        scratch_shapes=[pltpu.VMEM(keys_shape, BF16), pltpu.VMEM(keys_shape, BF16)],
        compiler_params=params,
        cost_estimate=pl.CostEstimate(
            flops=8 * peers * tok * blocks * rows * CHUNK, bytes_accessed=10 * tok * width,
            transcendentals=heads * tok * blocks * rows,
        ),
        name="memory_attention",
    )(gate_cols, -local_part.reshape(heads, HEAD_DIM), *got, *memory)
    arrived = across(replies[2:])
    core_back = send_xor(replies[1], PLANE, 1)
    core_back, arrived[0] = lax.optimization_barrier((core_back, arrived[0]))
    back = [replies[0], core_back] + forward(arrived)

    sums = sum_over(sum_over(part, "z"), "sa")
    for step in (1, 2, 4):
        sums = sums + send_xor(sums, PLANE, step)
    sums = jnp.sum(sums, axis=1)
    gate_grad = sums * gate * (1.0 - gate) / math.sqrt(tok * devices)

    out, d_query = pl.pallas_call(
        merge_kernel,
        out_shape=(whole, whole),
        in_specs=[vmem_spec] * (2 + peers),
        out_specs=(vmem_spec, vmem_spec),
        compiler_params=params,
        name="merge",
    )(local_mix, local_dq, *back)
    return (out, d_query, gate_grad)


def solution(mesh):
    seq, mem = mesh.devices.shape
    sb = min(seq, 4)
    fine = Mesh(mesh.devices.reshape(seq // sb, sb, mem // 2, 2), ALL)
    tokens = P(ALL, None)
    blocks = P(MEM, None)
    return jax.shard_map(
        body,
        mesh=fine,
        in_specs=(tokens, tokens, tokens, blocks, blocks, tokens, P(), tokens),
        out_specs=(tokens, tokens, P()),
        check_vma=False,
    )
```

```python
import functools
import math

import jax
import jax.numpy as jnp
from jax import lax
from jax.experimental import pallas as pl
from jax.experimental.pallas import tpu as pltpu
from jax.sharding import Mesh, PartitionSpec as P

HEAD_DIM = 128
PAIR = 2
CHUNK = PAIR * HEAD_DIM
TILE = 4
NEG = -1e30
LOG2E = math.log2(math.e)
MIB = 1024 * 1024
F32 = jnp.float32
BF16 = jnp.bfloat16
NT = (((1,), (1,)), ((), ()))
NN = (((1,), (0,)), ((), ()))
PLANE = ("sb", "core")
MEM = ("z", "core")
ALL = ("sa", "sb", "z", "core")


def dot(a, b, dims=NN):
    return lax.dot_general(a, b, dims, preferred_element_type=F32)


def head_cols(h):
    return slice(h * HEAD_DIM, (h + 1) * HEAD_DIM)


def chunk_columns(chunk):
    return pl.ds(pl.multiple_of(chunk * CHUNK, CHUNK), CHUNK)


def plane_index():
    return lax.axis_index("sb") * 2 + lax.axis_index("core")


def row_sums(x):
    high = x.astype(BF16)
    low = (x - high.astype(F32)).astype(BF16)
    return dot(jnp.concatenate([high, low], axis=1), jnp.ones((2 * HEAD_DIM, HEAD_DIM), BF16))


def packets_of(refs):
    own, core, *pairs = refs
    return [own, core] + [pair.at[lane] for pair in pairs for lane in range(2)]


def arrivals_of(refs):
    own, core, *pairs = refs
    return [own, core] + [pair.at[i % 2] for i, pair in enumerate(pairs)]


def prologue_kernel(
    blocks, mk_hbm, mv_hbm, q_hbm, g_hbm, ids_ref, mine_ref, theirs_ref, *refs
):
    *out_refs, mem_sems, in_sems = refs
    tok = q_hbm.shape[0]
    fetched, groups = ids_ref.shape
    chunk = plane_index()
    copies = [
        pltpu.make_async_copy(
            ref.at[:, chunk_columns(chunk ^ i)], out_ref.at[t], mem_sems.at[i, t]
        )
        for i, out_ref in enumerate((mine_ref, theirs_ref))
        for t, ref in enumerate((mk_hbm, mv_hbm))
    ]
    packets = packets_of(out_refs)
    for k, packet in enumerate(packets):
        for t, ref in enumerate((q_hbm, g_hbm)):
            span = slice(t * tok, (t + 1) * tok)
            copies.append(
                pltpu.make_async_copy(
                    ref.at[:, chunk_columns(chunk ^ k)], packet.at[span], in_sems.at[k, t]
                )
            )
    for copy in copies:
        copy.start()
    row = lax.broadcasted_iota(jnp.int32, (packets[0].shape[0] - 2 * tok, groups), 0)
    owner = lax.axis_index("z") * 2 + lax.axis_index("core")
    for core in range(2):
        hot = row >= blocks
        for t in range(fetched):
            hot = hot | (row == (ids_ref[t : t + 1, :] ^ owner ^ core))
        shun = jnp.where(hot, 0.0, 1.0).astype(BF16)
        for packet in packets[core::2]:
            packet[2 * tok :, :groups] = shun
    for copy in copies:
        copy.wait()


def join_kernel(mine_ref, other_ref, out_ref):
    out_ref[0] = mine_ref[...]
    out_ref[1] = other_ref[...]


def local_forward_kernel(scale, q_ref, k_ref, v_ref, g_ref, out_ref, prob_ref, part_ref):
    tok = q_ref.shape[0]
    heads = part_ref.shape[1]
    row = lax.broadcasted_iota(jnp.int32, (tok, tok), 0)
    col = lax.broadcasted_iota(jnp.int32, (tok, tok), 1)
    causal = row >= col
    s = [dot(q_ref[:, head_cols(h)], k_ref[:, head_cols(h)], NT) for h in range(heads)]
    s = [jnp.where(causal, x, NEG) for x in s]
    e = [jnp.exp2((x - jnp.max(x, axis=1, keepdims=True)) * (scale * LOG2E)) for x in s]
    p = [x * (1.0 / row_sums(x)) for x in e]
    p = [x.astype(BF16) for x in p]
    for h in range(heads):
        cols = head_cols(h)
        o = dot(p[h], v_ref[:, cols])
        prob_ref[h] = p[h]
        out_ref[:, cols] = o
        part_ref[0, h : h + 1, :] = jnp.sum(g_ref[:, cols].astype(F32) * o, axis=0, keepdims=True)


def local_backward_kernel(scale, k_ref, v_ref, g_ref, gate_ref, out_ref, prob_ref, lo_ref, dq_ref):
    heads = prob_ref.shape[0]
    for h in range(heads):
        shut = 1.0 - gate_ref[:, head_cols(h)]
        lo_ref[:, head_cols(h)] = (shut * out_ref[:, head_cols(h)]).astype(BF16)
    dout = [
        ((1.0 - gate_ref[:, head_cols(h)]) * g_ref[:, head_cols(h)].astype(F32)).astype(BF16)
        for h in range(heads)
    ]
    delta = [row_sums(dout[h].astype(F32) * out_ref[:, head_cols(h)]) for h in range(heads)]
    dp = [dot(dout[h], v_ref[:, head_cols(h)], NT) for h in range(heads)]
    for h in range(heads):
        ds = (prob_ref[h].astype(F32) * (dp[h] - delta[h])).astype(BF16)
        dq_ref[:, head_cols(h)] = (dot(ds, k_ref[:, head_cols(h)]) * scale).astype(BF16)


def tile_rows(packets, first, start, count, cols):
    return jnp.concatenate(
        [packets[first + t][start : start + count, cols] for t in range(TILE)], axis=0
    )


def gate_of(gate_ref, h):
    return gate_ref[:, chunk_columns(plane_index())][:, head_cols(h)]


def backward(scale, e, dout, delta, inv, k_ref, v_ref, h):
    keys = k_ref.shape[1]
    dp = dot(dout, v_ref[h, :, :HEAD_DIM], NT)
    delta = jnp.concatenate([delta] * (keys // HEAD_DIM), axis=1)
    ds = (e.astype(F32) * (dp - delta)).astype(BF16)
    return (dot(ds, k_ref[h, :, :HEAD_DIM]) * (inv * scale)).astype(BF16)


def attend_kernel(scale, groups, peers, gate_ref, before_ref, *refs):
    *refs, part_ref, k_all, v_all = refs
    got, refs = arrivals_of(refs[:peers]), refs[peers:]
    pairs = peers // 2 - 1
    mem_refs, back = refs[: -pairs - 2], packets_of(refs[-pairs - 2 :])
    rows = mem_refs[0].shape[2]
    heads = before_ref.shape[0]
    tok = back[0].shape[0] // 2
    extra = got[0].shape[0] - 2 * tok
    lane = lax.broadcasted_iota(jnp.int32, (rows, HEAD_DIM), 1)
    for h in range(PAIR):
        for b in range(2 * len(mem_refs)):
            ref = mem_refs[b // 2]
            span = slice(b * rows, (b + 1) * rows)
            k_all[h, span, :HEAD_DIM] = ref[b % 2, 0, :, head_cols(h)]
            k_all[h, span, HEAD_DIM:] = jnp.where(lane == b, NEG, 0.0).astype(BF16)
            v_all[h, span, :HEAD_DIM] = ref[b % 2, 1, :, head_cols(h)]
            v_all[h, span, HEAD_DIM:] = jnp.ones((rows, HEAD_DIM), BF16)
    spread = (
        lax.broadcasted_iota(jnp.int32, (tok, groups), 0) // (tok // groups)
        == lax.broadcasted_iota(jnp.int32, (tok, groups), 1)
    )
    spread = jnp.where(spread, 1.0, 0.0).astype(BF16)
    pad = jnp.zeros((HEAD_DIM - extra, groups), BF16)

    units = [(first, h) for first in range(0, peers, TILE) for h in range(PAIR)]
    shunned, scores, weights, parts = {}, {}, {}, [0.0] * PAIR
    for step in range(len(units) + 2):
        if step < len(units):
            first, h = units[step]
            if first not in shunned:
                shun = [
                    jnp.concatenate([got[first + t][2 * tok :, :groups], pad], axis=0)
                    for t in range(TILE)
                ]
                shunned[first] = jnp.concatenate(
                    [dot(spread, x, NT).astype(BF16) for x in shun], axis=0
                )
            q = tile_rows(got, first, 0, tok, head_cols(h))
            scores[step] = dot(jnp.concatenate([q, shunned[first]], axis=1), k_all[h], NT)
        if 1 <= step <= len(units):
            u = step - 1
            first, h = units[u]
            gate = gate_of(gate_ref, h)
            s = scores.pop(u)
            peak = jnp.max(s, axis=1, keepdims=True)
            e = jnp.exp2((s - peak) * (scale * LOG2E)).astype(BF16)
            o = dot(e, v_all[h])
            inv = 1.0 / o[:, HEAD_DIM:]
            o = o[:, :HEAD_DIM] * inv
            g32 = tile_rows(got, first, tok, tok, head_cols(h)).astype(F32)
            dout = (gate * g32).astype(BF16)
            delta = row_sums(dout.astype(F32) * o)
            mixed = (gate * o).astype(BF16)
            for t in range(TILE):
                back[first + t][:tok, head_cols(h)] = mixed[t * tok : (t + 1) * tok]
            parts[h] = parts[h] + jnp.sum(g32 * o, axis=0, keepdims=True)
            weights[u] = (e, dout, delta, inv)
        if 2 <= step:
            u = step - 2
            first, h = units[u]
            dq = backward(scale, *weights.pop(u), k_all, v_all, h)
            for t in range(TILE):
                back[first + t][tok : 2 * tok, head_cols(h)] = dq[t * tok : (t + 1) * tok]

    head = lax.broadcasted_iota(jnp.int32, (heads, HEAD_DIM), 0)
    total = before_ref[...]
    for h in range(PAIR):
        total = total + jnp.where(head == plane_index() * PAIR + h, parts[h], 0.0)
    part_ref[...] = total


def merge_kernel(lo_ref, ldq_ref, *refs):
    *back_refs, out_ref, dq_ref = refs
    back_refs = arrivals_of(back_refs)
    tok = lo_ref.shape[0]
    chunk = plane_index()
    for k, back_ref in enumerate(back_refs):
        cols = chunk_columns(chunk ^ k)
        for t, (ref, local_ref) in enumerate(((out_ref, lo_ref), (dq_ref, ldq_ref))):
            arrived = back_ref[t * tok : (t + 1) * tok].astype(F32)
            ref[:, cols] = (arrived + local_ref[:, cols].astype(F32)).astype(BF16)


def send_xor(array, axes, k):
    return lax.ppermute(array, axes, [(i, i ^ k) for i in range(lax.axis_size(axes))])


def spread_along(array, axis, ready):
    held = {0: array}
    step = lax.axis_size(axis) // 2
    while step:
        for k in sorted(held):
            source = held[k]
            if k and step == 1:
                source, held[1], ready = lax.optimization_barrier((source, held[1], ready))
            held[k + step] = send_xor(source, axis, step)
        step //= 2
    return held, ready


def across(pairs):
    order = reversed(range(len(pairs)))
    return [send_xor(pairs[i], PLANE, 2 * i + 2) for i in order][::-1]


def forward(pairs):
    return [x for pair in pairs for x in (pair, send_xor(pair, PLANE, 1))]


def sum_over(array, axis):
    arrived = [send_xor(array, axis, k) for k in range(1, lax.axis_size(axis))]
    return functools.reduce(jnp.add, arrived, array)


def body(query, key, value, mem_key, mem_value, block_ids, gate_logit, d_out):
    tok, width = query.shape
    heads = gate_logit.shape[0]
    scale = HEAD_DIM ** (-0.5)
    rows = mem_key.shape[0]
    groups = block_ids.shape[0]
    blocks = lax.axis_size(MEM)
    peers = width // CHUNK
    devices = lax.axis_size(ALL)

    params = pltpu.CompilerParams(vmem_limit_bytes=(6 + 5 * blocks // 4) * MIB)
    alone = pltpu.CompilerParams(vmem_limit_bytes=60 * MIB)
    hbm_spec = pl.BlockSpec(memory_space=pltpu.HBM)
    vmem_spec = pl.BlockSpec(memory_space=pltpu.VMEM)
    packet = jax.ShapeDtypeStruct((2 * tok + max(16, blocks), CHUNK), BF16)
    pairs = peers // 2 - 1
    pair_packet = jax.ShapeDtypeStruct((2,) + packet.shape, BF16)
    chunk_shape = jax.ShapeDtypeStruct((2, rows, CHUNK), BF16)
    mine, theirs, *send = pl.pallas_call(
        functools.partial(prologue_kernel, blocks),
        out_shape=(chunk_shape,) * 2 + (packet,) * 2 + (pair_packet,) * pairs,
        in_specs=[hbm_spec] * 4 + [vmem_spec],
        out_specs=(vmem_spec,) * (4 + pairs),
        scratch_shapes=[pltpu.SemaphoreType.DMA((2, 2)), pltpu.SemaphoreType.DMA((peers, 2))],
        compiler_params=alone,
        name="chunks",
    )(mem_key, mem_value, query, d_out, jnp.transpose(block_ids))
    both = pl.pallas_call(
        join_kernel,
        out_shape=jax.ShapeDtypeStruct((2,) + chunk_shape.shape, BF16),
        in_specs=[vmem_spec] * 2,
        out_specs=vmem_spec,
        compiler_params=params,
        name="join_cores",
    )(mine, send_xor(theirs, "core", 1))

    gate = jax.nn.sigmoid(gate_logit)
    gate_cols = jnp.repeat(gate, HEAD_DIM)[None, :]
    steps = 4
    step_heads = heads // steps
    col_spec = pl.BlockSpec((tok, step_heads * HEAD_DIM), lambda j: (0, j))
    prob_spec = pl.BlockSpec((step_heads, tok, tok), lambda j: (j, 0, 0))
    local_out, local_prob, local_part = pl.pallas_call(
        functools.partial(local_forward_kernel, scale),
        grid=(steps,),
        out_shape=(
            jax.ShapeDtypeStruct((tok, width), F32),
            jax.ShapeDtypeStruct((heads, tok, tok), BF16),
            jax.ShapeDtypeStruct((steps, step_heads, HEAD_DIM), F32),
        ),
        in_specs=[col_spec] * 4,
        out_specs=(
            col_spec,
            prob_spec,
            pl.BlockSpec((1, step_heads, HEAD_DIM), lambda j: (j, 0, 0)),
        ),
        compiler_params=params,
        cost_estimate=pl.CostEstimate(
            flops=4 * heads * tok * tok * HEAD_DIM, bytes_accessed=12 * tok * width,
            transcendentals=heads * tok * tok,
        ),
        name="local_forward",
    )(query, key, value, d_out)

    both, pair_packets = lax.optimization_barrier((both, send[2:]))
    arrived = across(pair_packets)
    spread, (arrived, local_part) = spread_along(both, "z", (arrived, local_part))
    got = [send[0], send_xor(send[1], PLANE, 1)] + forward(arrived)
    memory = [spread[k] for k in range(blocks // 2)]

    whole = jax.ShapeDtypeStruct((tok, width), BF16)
    local_mix, local_dq = pl.pallas_call(
        functools.partial(local_backward_kernel, scale),
        grid=(steps,),
        out_shape=(whole, whole),
        in_specs=[col_spec] * 3
        + [pl.BlockSpec((1, step_heads * HEAD_DIM), lambda j: (0, j)), col_spec, prob_spec],
        out_specs=(col_spec, col_spec),
        compiler_params=params,
        cost_estimate=pl.CostEstimate(
            flops=4 * heads * tok * tok * HEAD_DIM, bytes_accessed=16 * tok * width,
            transcendentals=0,
        ),
        name="local_backward",
    )(key, value, d_out, gate_cols, local_out, local_prob)
    memory, local_mix, local_dq = lax.optimization_barrier((memory, local_mix, local_dq))

    keys_shape = (PAIR, blocks * rows, CHUNK)

    reply = jax.ShapeDtypeStruct((2 * tok, CHUNK), BF16)
    pair_reply = jax.ShapeDtypeStruct((2,) + reply.shape, BF16)
    *replies, part = pl.pallas_call(
        functools.partial(attend_kernel, scale, groups, peers),
        out_shape=(reply,) * 2
        + (pair_reply,) * pairs
        + (jax.ShapeDtypeStruct((heads, HEAD_DIM), F32),),
        in_specs=[vmem_spec] * (2 + peers + blocks // 2),
        out_specs=(vmem_spec,) * (3 + pairs),
        scratch_shapes=[pltpu.VMEM(keys_shape, BF16), pltpu.VMEM(keys_shape, BF16)],
        compiler_params=params,
        cost_estimate=pl.CostEstimate(
            flops=8 * peers * tok * blocks * rows * CHUNK, bytes_accessed=10 * tok * width,
            transcendentals=heads * tok * blocks * rows,
        ),
        name="memory_attention",
    )(gate_cols, -local_part.reshape(heads, HEAD_DIM), *got, *memory)
    arrived = across(replies[2:])
    core_back = send_xor(replies[1], PLANE, 1)
    core_back, arrived[0] = lax.optimization_barrier((core_back, arrived[0]))
    back = [replies[0], core_back] + forward(arrived)

    sums = sum_over(sum_over(part, "z"), "sa")
    for step in (1, 2, 4):
        sums = sums + send_xor(sums, PLANE, step)
    sums = jnp.sum(sums, axis=1)
    gate_grad = sums * gate * (1.0 - gate) / math.sqrt(tok * devices)

    out, d_query = pl.pallas_call(
        merge_kernel,
        out_shape=(whole, whole),
        in_specs=[vmem_spec] * (2 + peers),
        out_specs=(vmem_spec, vmem_spec),
        compiler_params=params,
        name="merge",
    )(local_mix, local_dq, *back)
    return (out, d_query, gate_grad)


def solution(mesh):
    seq, mem = mesh.devices.shape
    sb = min(seq, 4)
    fine = Mesh(mesh.devices.reshape(seq // sb, sb, mem // 2, 2), ALL)
    tokens = P(ALL, None)
    blocks = P(MEM, None)
    return jax.shard_map(
        body,
        mesh=fine,
        in_specs=(tokens, tokens, tokens, blocks, blocks, tokens, P(), tokens),
        out_specs=(tokens, tokens, P()),
        check_vma=False,
    )
```

```python
import functools
import math

import jax
import jax.numpy as jnp
from jax import lax
from jax.experimental import pallas as pl
from jax.experimental.pallas import tpu as pltpu
from jax.sharding import Mesh, PartitionSpec as P

HEAD_DIM = 128
PAIR = 2
CHUNK = PAIR * HEAD_DIM
TILE = 8
NEG = -1e30
LOG2E = math.log2(math.e)
MIB = 1024 * 1024
F32 = jnp.float32
BF16 = jnp.bfloat16
NT = (((1,), (1,)), ((), ()))
NN = (((1,), (0,)), ((), ()))
PLANE = ("sb", "core")
MEM = ("z", "core")
ALL = ("sa", "sb", "z", "core")


def dot(a, b, dims=NN):
    return lax.dot_general(a, b, dims, preferred_element_type=F32)


def head_cols(h):
    return slice(h * HEAD_DIM, (h + 1) * HEAD_DIM)


def chunk_columns(chunk):
    return pl.ds(pl.multiple_of(chunk * CHUNK, CHUNK), CHUNK)


def plane_index():
    return lax.axis_index("sb") * 2 + lax.axis_index("core")


def row_sums(x):
    high = x.astype(BF16)
    low = (x - high.astype(F32)).astype(BF16)
    return dot(jnp.concatenate([high, low], axis=1), jnp.ones((2 * HEAD_DIM, HEAD_DIM), BF16))


def packets_of(refs):
    own, core, *pairs = refs
    return [own, core] + [pair.at[lane] for pair in pairs for lane in range(2)]


def arrivals_of(refs):
    own, core, *pairs = refs
    return [own, core] + [pair.at[i % 2] for i, pair in enumerate(pairs)]


def prologue_kernel(
    blocks, mk_hbm, mv_hbm, q_hbm, g_hbm, ids_ref, mine_ref, theirs_ref, *refs
):
    *out_refs, mem_sems, in_sems = refs
    tok = q_hbm.shape[0]
    fetched, groups = ids_ref.shape
    chunk = plane_index()
    copies = [
        pltpu.make_async_copy(
            ref.at[:, chunk_columns(chunk ^ i)], out_ref.at[t], mem_sems.at[i, t]
        )
        for i, out_ref in enumerate((mine_ref, theirs_ref))
        for t, ref in enumerate((mk_hbm, mv_hbm))
    ]
    for k, packet in enumerate(out_refs):
        for t, ref in enumerate((q_hbm, g_hbm)):
            span = slice(t * tok, (t + 1) * tok)
            copies.append(
                pltpu.make_async_copy(
                    ref.at[:, chunk_columns(chunk ^ k)], packet.at[span], in_sems.at[k, t]
                )
            )
    for copy in copies:
        copy.start()
    row = lax.broadcasted_iota(jnp.int32, (out_refs[0].shape[0] - 2 * tok, groups), 0)
    owner = lax.axis_index("z") * 2 + lax.axis_index("core")
    for core in range(2):
        hot = row >= blocks
        for t in range(fetched):
            hot = hot | (row == (ids_ref[t : t + 1, :] ^ owner ^ core))
        shun = jnp.where(hot, 0.0, 1.0).astype(BF16)
        for packet in out_refs[core::2]:
            packet[2 * tok :, :groups] = shun
    for copy in copies:
        copy.wait()


def join_kernel(mine_ref, other_ref, out_ref):
    out_ref[0] = mine_ref[...]
    out_ref[1] = other_ref[...]


def local_forward_kernel(scale, q_ref, k_ref, v_ref, g_ref, out_ref, prob_ref, part_ref):
    tok = q_ref.shape[0]
    heads = part_ref.shape[1]
    row = lax.broadcasted_iota(jnp.int32, (tok, tok), 0)
    col = lax.broadcasted_iota(jnp.int32, (tok, tok), 1)
    causal = row >= col
    s = [dot(q_ref[:, head_cols(h)], k_ref[:, head_cols(h)], NT) for h in range(heads)]
    s = [jnp.where(causal, x, NEG) for x in s]
    e = [jnp.exp2((x - jnp.max(x, axis=1, keepdims=True)) * (scale * LOG2E)) for x in s]
    p = [x * (1.0 / row_sums(x)) for x in e]
    p = [x.astype(BF16) for x in p]
    for h in range(heads):
        cols = head_cols(h)
        o = dot(p[h], v_ref[:, cols])
        prob_ref[h] = p[h]
        out_ref[:, cols] = o
        part_ref[0, h : h + 1, :] = jnp.sum(g_ref[:, cols].astype(F32) * o, axis=0, keepdims=True)


def local_backward_kernel(scale, k_ref, v_ref, g_ref, gate_ref, out_ref, prob_ref, lo_ref, dq_ref):
    heads = prob_ref.shape[0]
    for h in range(heads):
        shut = 1.0 - gate_ref[:, head_cols(h)]
        lo_ref[:, head_cols(h)] = (shut * out_ref[:, head_cols(h)]).astype(BF16)
    dout = [
        ((1.0 - gate_ref[:, head_cols(h)]) * g_ref[:, head_cols(h)].astype(F32)).astype(BF16)
        for h in range(heads)
    ]
    delta = [row_sums(dout[h].astype(F32) * out_ref[:, head_cols(h)]) for h in range(heads)]
    dp = [dot(dout[h], v_ref[:, head_cols(h)], NT) for h in range(heads)]
    for h in range(heads):
        ds = (prob_ref[h].astype(F32) * (dp[h] - delta[h])).astype(BF16)
        dq_ref[:, head_cols(h)] = (dot(ds, k_ref[:, head_cols(h)]) * scale).astype(BF16)


def tile_rows(packets, first, start, count, cols):
    return jnp.concatenate(
        [packets[first + t][start : start + count, cols] for t in range(TILE)], axis=0
    )


def gate_of(gate_ref, h):
    return gate_ref[:, chunk_columns(plane_index())][:, head_cols(h)]


def backward(scale, e, dout, delta, inv, k_ref, v_ref, h):
    keys = k_ref.shape[1]
    dp = dot(dout, v_ref[h, :, :HEAD_DIM], NT)
    delta = jnp.concatenate([delta] * (keys // HEAD_DIM), axis=1)
    ds = (e.astype(F32) * (dp - delta)).astype(BF16)
    return (dot(ds, k_ref[h, :, :HEAD_DIM]) * (inv * scale)).astype(BF16)


def attend_kernel(scale, groups, peers, gate_ref, before_ref, *refs):
    *refs, part_ref, k_all, v_all = refs
    got, refs = refs[:peers], refs[peers:]
    pairs = peers // 2 - 1
    mem_refs, back = refs[: -pairs - 2], packets_of(refs[-pairs - 2 :])
    rows = mem_refs[0].shape[2]
    heads = before_ref.shape[0]
    tok = back[0].shape[0] // 2
    extra = got[0].shape[0] - 2 * tok
    lane = lax.broadcasted_iota(jnp.int32, (rows, HEAD_DIM), 1)
    for h in range(PAIR):
        for b in range(2 * len(mem_refs)):
            ref = mem_refs[b // 2]
            span = slice(b * rows, (b + 1) * rows)
            k_all[h, span, :HEAD_DIM] = ref[b % 2, 0, :, head_cols(h)]
            k_all[h, span, HEAD_DIM:] = jnp.where(lane == b, NEG, 0.0).astype(BF16)
            v_all[h, span, :HEAD_DIM] = ref[b % 2, 1, :, head_cols(h)]
            v_all[h, span, HEAD_DIM:] = jnp.ones((rows, HEAD_DIM), BF16)
    spread = (
        lax.broadcasted_iota(jnp.int32, (tok, groups), 0) // (tok // groups)
        == lax.broadcasted_iota(jnp.int32, (tok, groups), 1)
    )
    spread = jnp.where(spread, 1.0, 0.0).astype(BF16)
    pad = jnp.zeros((HEAD_DIM - extra, groups), BF16)

    units = [(first, h) for first in range(0, peers, TILE) for h in range(PAIR)]
    shunned, scores, weights, parts = {}, {}, {}, [0.0] * PAIR
    for step in range(len(units) + 2):
        if step < len(units):
            first, h = units[step]
            if first not in shunned:
                shun = [
                    jnp.concatenate([got[first + t][2 * tok :, :groups], pad], axis=0)
                    for t in range(TILE)
                ]
                shunned[first] = jnp.concatenate(
                    [dot(spread, x, NT).astype(BF16) for x in shun], axis=0
                )
            q = tile_rows(got, first, 0, tok, head_cols(h))
            scores[step] = dot(jnp.concatenate([q, shunned[first]], axis=1), k_all[h], NT)
        if 1 <= step <= len(units):
            u = step - 1
            first, h = units[u]
            gate = gate_of(gate_ref, h)
            s = scores.pop(u)
            peak = jnp.max(s, axis=1, keepdims=True)
            e = jnp.exp2((s - peak) * (scale * LOG2E)).astype(BF16)
            o = dot(e, v_all[h])
            inv = 1.0 / o[:, HEAD_DIM:]
            o = o[:, :HEAD_DIM] * inv
            g32 = tile_rows(got, first, tok, tok, head_cols(h)).astype(F32)
            dout = (gate * g32).astype(BF16)
            delta = row_sums(dout.astype(F32) * o)
            mixed = (gate * o).astype(BF16)
            for t in range(TILE):
                back[first + t][:tok, head_cols(h)] = mixed[t * tok : (t + 1) * tok]
            parts[h] = parts[h] + jnp.sum(g32 * o, axis=0, keepdims=True)
            weights[u] = (e, dout, delta, inv)
        if 2 <= step:
            u = step - 2
            first, h = units[u]
            dq = backward(scale, *weights.pop(u), k_all, v_all, h)
            for t in range(TILE):
                back[first + t][tok : 2 * tok, head_cols(h)] = dq[t * tok : (t + 1) * tok]

    head = lax.broadcasted_iota(jnp.int32, (heads, HEAD_DIM), 0)
    total = before_ref[...]
    for h in range(PAIR):
        total = total + jnp.where(head == plane_index() * PAIR + h, parts[h], 0.0)
    part_ref[...] = total


def merge_kernel(lo_ref, ldq_ref, *refs):
    *back_refs, out_ref, dq_ref = refs
    back_refs = arrivals_of(back_refs)
    tok = lo_ref.shape[0]
    chunk = plane_index()
    for k, back_ref in enumerate(back_refs):
        cols = chunk_columns(chunk ^ k)
        for t, (ref, local_ref) in enumerate(((out_ref, lo_ref), (dq_ref, ldq_ref))):
            arrived = back_ref[t * tok : (t + 1) * tok].astype(F32)
            ref[:, cols] = (arrived + local_ref[:, cols].astype(F32)).astype(BF16)


def send_xor(array, axes, k):
    return lax.ppermute(array, axes, [(i, i ^ k) for i in range(lax.axis_size(axes))])


def spread_along(array, axis, ready):
    held = {0: array}
    step = lax.axis_size(axis) // 2
    while step:
        for k in sorted(held):
            source = held[k]
            if k and step == 1:
                source, held[1], ready = lax.optimization_barrier((source, held[1], ready))
            held[k + step] = send_xor(source, axis, step)
        step //= 2
    return held, ready


def across(pairs):
    order = reversed(range(len(pairs)))
    return [send_xor(pairs[i], PLANE, 2 * i + 2) for i in order][::-1]


def forward(pairs):
    return [x for pair in pairs for x in (pair, send_xor(pair, PLANE, 1))]


def sum_over(array, axis):
    arrived = [send_xor(array, axis, k) for k in range(1, lax.axis_size(axis))]
    return functools.reduce(jnp.add, arrived, array)


def body(query, key, value, mem_key, mem_value, block_ids, gate_logit, d_out):
    tok, width = query.shape
    heads = gate_logit.shape[0]
    scale = HEAD_DIM ** (-0.5)
    rows = mem_key.shape[0]
    groups = block_ids.shape[0]
    blocks = lax.axis_size(MEM)
    peers = width // CHUNK
    devices = lax.axis_size(ALL)

    params = pltpu.CompilerParams(vmem_limit_bytes=(6 + 5 * blocks // 4) * MIB)
    alone = pltpu.CompilerParams(vmem_limit_bytes=60 * MIB)
    hbm_spec = pl.BlockSpec(memory_space=pltpu.HBM)
    vmem_spec = pl.BlockSpec(memory_space=pltpu.VMEM)
    packet = jax.ShapeDtypeStruct((2 * tok + max(16, blocks), CHUNK), BF16)
    pairs = peers // 2 - 1
    chunk_shape = jax.ShapeDtypeStruct((2, rows, CHUNK), BF16)
    mine, theirs, *send = pl.pallas_call(
        functools.partial(prologue_kernel, blocks),
        out_shape=(chunk_shape,) * 2 + (packet,) * peers,
        in_specs=[hbm_spec] * 4 + [vmem_spec],
        out_specs=(vmem_spec,) * (2 + peers),
        scratch_shapes=[pltpu.SemaphoreType.DMA((2, 2)), pltpu.SemaphoreType.DMA((peers, 2))],
        compiler_params=alone,
        name="chunks",
    )(mem_key, mem_value, query, d_out, jnp.transpose(block_ids))
    both = pl.pallas_call(
        join_kernel,
        out_shape=jax.ShapeDtypeStruct((2,) + chunk_shape.shape, BF16),
        in_specs=[vmem_spec] * 2,
        out_specs=vmem_spec,
        compiler_params=params,
        name="join_cores",
    )(mine, send_xor(theirs, "core", 1))

    gate = jax.nn.sigmoid(gate_logit)
    gate_cols = jnp.repeat(gate, HEAD_DIM)[None, :]
    steps = 4
    step_heads = heads // steps
    col_spec = pl.BlockSpec((tok, step_heads * HEAD_DIM), lambda j: (0, j))
    prob_spec = pl.BlockSpec((step_heads, tok, tok), lambda j: (j, 0, 0))
    local_out, local_prob, local_part = pl.pallas_call(
        functools.partial(local_forward_kernel, scale),
        grid=(steps,),
        out_shape=(
            jax.ShapeDtypeStruct((tok, width), F32),
            jax.ShapeDtypeStruct((heads, tok, tok), BF16),
            jax.ShapeDtypeStruct((steps, step_heads, HEAD_DIM), F32),
        ),
        in_specs=[col_spec] * 4,
        out_specs=(
            col_spec,
            prob_spec,
            pl.BlockSpec((1, step_heads, HEAD_DIM), lambda j: (j, 0, 0)),
        ),
        compiler_params=params,
        cost_estimate=pl.CostEstimate(
            flops=4 * heads * tok * tok * HEAD_DIM, bytes_accessed=12 * tok * width,
            transcendentals=heads * tok * tok,
        ),
        name="local_forward",
    )(query, key, value, d_out)

    got = list(send)
    for k in (6, 7, 5, 4, 2, 3, 1):
        got[k] = send_xor(send[k], PLANE, k)
    spread, (got[5:], local_part) = spread_along(both, "z", (got[5:], local_part))
    memory = [spread[k] for k in range(blocks // 2)]

    whole = jax.ShapeDtypeStruct((tok, width), BF16)
    local_mix, local_dq = pl.pallas_call(
        functools.partial(local_backward_kernel, scale),
        grid=(steps,),
        out_shape=(whole, whole),
        in_specs=[col_spec] * 3
        + [pl.BlockSpec((1, step_heads * HEAD_DIM), lambda j: (0, j)), col_spec, prob_spec],
        out_specs=(col_spec, col_spec),
        compiler_params=params,
        cost_estimate=pl.CostEstimate(
            flops=4 * heads * tok * tok * HEAD_DIM, bytes_accessed=16 * tok * width,
            transcendentals=0,
        ),
        name="local_backward",
    )(key, value, d_out, gate_cols, local_out, local_prob)
    memory, local_mix, local_dq = lax.optimization_barrier((memory, local_mix, local_dq))

    keys_shape = (PAIR, blocks * rows, CHUNK)

    reply = jax.ShapeDtypeStruct((2 * tok, CHUNK), BF16)
    pair_reply = jax.ShapeDtypeStruct((2,) + reply.shape, BF16)
    *replies, part = pl.pallas_call(
        functools.partial(attend_kernel, scale, groups, peers),
        out_shape=(reply,) * 2
        + (pair_reply,) * pairs
        + (jax.ShapeDtypeStruct((heads, HEAD_DIM), F32),),
        in_specs=[vmem_spec] * (2 + peers + blocks // 2),
        out_specs=(vmem_spec,) * (3 + pairs),
        scratch_shapes=[pltpu.VMEM(keys_shape, BF16), pltpu.VMEM(keys_shape, BF16)],
        compiler_params=params,
        cost_estimate=pl.CostEstimate(
            flops=8 * peers * tok * blocks * rows * CHUNK, bytes_accessed=10 * tok * width,
            transcendentals=heads * tok * blocks * rows,
        ),
        name="memory_attention",
    )(gate_cols, -local_part.reshape(heads, HEAD_DIM), *got, *memory)
    arrived = across(replies[2:])
    core_back = send_xor(replies[1], PLANE, 1)
    core_back, arrived[0] = lax.optimization_barrier((core_back, arrived[0]))
    back = [replies[0], core_back] + forward(arrived)

    sums = sum_over(sum_over(part, "z"), "sa")
    for step in (1, 2, 4):
        sums = sums + send_xor(sums, PLANE, step)
    sums = jnp.sum(sums, axis=1)
    gate_grad = sums * gate * (1.0 - gate) / math.sqrt(tok * devices)

    out, d_query = pl.pallas_call(
        merge_kernel,
        out_shape=(whole, whole),
        in_specs=[vmem_spec] * (2 + peers),
        out_specs=(vmem_spec, vmem_spec),
        compiler_params=params,
        name="merge",
    )(local_mix, local_dq, *back)
    return (out, d_query, gate_grad)


def solution(mesh):
    seq, mem = mesh.devices.shape
    sb = min(seq, 4)
    fine = Mesh(mesh.devices.reshape(seq // sb, sb, mem // 2, 2), ALL)
    tokens = P(ALL, None)
    blocks = P(MEM, None)
    return jax.shard_map(
        body,
        mesh=fine,
        in_specs=(tokens, tokens, tokens, blocks, blocks, tokens, P(), tokens),
        out_specs=(tokens, tokens, P()),
        check_vma=False,
    )
```
